128 devices in a mesh: row: 8 (over y, core), col: 16 (over z, x).
Axes of the slice: x: 4, y: 4, z: 4, core: 2. Of those that a mesh axis runs over, the one named last changes fastest.
Arguments:
- factor: float32 [8, 8, 256, 4, 16, 256], P(None, 'row', None, None, 'col'), as said below
- adjoint: float32 [8, 8, 256, 4, 16, 256], P(None, 'row', None, None, 'col'), may hold values from -6 to 6
Outputs:
- adjoint_out: float32 [8, 8, 256, 4, 16, 256], P(None, 'row', None, None, 'col')
The draws below stay inside these ranges and needn't reach their ends.
Inputs may be any that keep to these rules, and one draw needn't show every extreme that they name: factor is lower triangular with diagonal entries between 1 and 2.
All inputs are finite; a program needn't handle non-finite values.
Results may differ from the reference program's by a relative error of at most 0.00011.
Values sent between devices are 32-bit elements; how exact they have to be, the bound alone decides.
A program may use at most 192 MiB of HBM per device.

```python
import jax
import jax.numpy as jnp
from jax import lax

BLOCK = 256
BLOCKS_ACROSS = 4
GRID_ROWS = 8
GRID_COLS = 16
BLOCKS_DOWN = 8
ORDER = 16384


def draw_factor(key, part):
    key = jax.random.fold_in(key, 11)
    key_base, key_pivot = jax.random.split(key, 2)
    shape = (BLOCKS_DOWN, GRID_ROWS, BLOCK, BLOCKS_ACROSS, GRID_COLS, BLOCK)
    row_blocks = jnp.arange(BLOCKS_DOWN)[:, None] * GRID_ROWS + jnp.arange(GRID_ROWS)[None, :]
    row_ids = (row_blocks[:, :, None] * BLOCK + jnp.arange(BLOCK)[None, None, :]).reshape(BLOCKS_DOWN, GRID_ROWS, BLOCK, 1, 1, 1)
    col_blocks = jnp.arange(BLOCKS_ACROSS)[:, None] * GRID_COLS + jnp.arange(GRID_COLS)[None, :]
    col_ids = (col_blocks[:, :, None] * BLOCK + jnp.arange(BLOCK)[None, None, :]).reshape(1, 1, 1, BLOCKS_ACROSS, GRID_COLS, BLOCK)
    same_block = row_ids // BLOCK == col_ids // BLOCK
    base = jax.random.normal(key_base, shape, jnp.float32)
    far_part = base * ORDER ** (-0.5)
    near_part = base * (0.5 * BLOCK ** (-0.5))
    diagonal = jax.random.uniform(key_pivot, shape, jnp.float32, 1.0, 2.0)
    lower_part = jnp.where(same_block, near_part, far_part)
    value = jnp.where(row_ids == col_ids, diagonal, jnp.where(row_ids > col_ids, lower_part, 0.0))
    return value.astype(jnp.float32)


def block_scale(key, shape, cuts, smallest, high):
    factor_of = 1.0
    for dim, parts in cuts:
        draws = jax.random.uniform(jax.random.fold_in(jax.random.fold_in(key, 6), dim), (parts,), jnp.float32, smallest / len(cuts), high / len(cuts))
        factor_of = factor_of * jnp.repeat(jnp.exp(draws), shape[dim] // parts).reshape((-1,) + (1,) * (len(shape) - 1 - dim))
    return factor_of


def centred(key, dims, spread, limit, pieces=(), held_as=jnp.bfloat16):
    values = jax.random.normal(key, dims, jnp.float32) * spread
    if len(pieces) > 0:
        values = block_scale(key, dims, pieces, -0.22, 0.18) * values
    return jnp.clip(values, min=-limit, max=limit).astype(held_as)


def setup_inputs(seed: int = 0) -> dict:
    key_of = jax.random.split(jax.random.key(seed), 3)
    factor = draw_factor(jax.random.fold_in(key_of[2], 71), 0)
    adjoint = centred(key_of[1], (BLOCKS_DOWN, GRID_ROWS, BLOCK, BLOCKS_ACROSS, GRID_COLS, BLOCK), 1.0, 6.0, ((1, 8), (4, 16)), jnp.float32)
    return dict(factor=factor, adjoint=adjoint)


precise = lax.Precision.HIGHEST

def halve_diag(matrix):
    extent = matrix.shape[0]
    keep_mask = jnp.tril(jnp.ones((extent, extent), jnp.float32)) - 0.5 * jnp.eye(extent, dtype=jnp.float32)
    return matrix * keep_mask

def cholesky_adjoint(pivot_block, target_adjoint):
    inner_part = halve_diag(jnp.dot(pivot_block.T.astype(jnp.float32), target_adjoint.astype(jnp.float32), precision=precise, preferred_element_type=jnp.float32))
    left_side = jax.scipy.linalg.solve_triangular(pivot_block, inner_part, trans=1, lower=True)
    both_sides = jax.scipy.linalg.solve_triangular(pivot_block, left_side.T, trans=1, lower=True).T
    return halve_diag(both_sides)

def reference(factor, adjoint):
    factor_full = factor.reshape(ORDER, ORDER)
    result = jnp.tril(adjoint.reshape(ORDER, ORDER))
    for target in (1, 0):
        first_row = target * BLOCK
        end_row = first_row + BLOCK
        pivot_block = factor_full[first_row:end_row, first_row:end_row]
        panel_cols = factor_full[end_row:, first_row:end_row]
        trailing = result[end_row:, end_row:]
        pushed = jnp.dot(trailing.astype(jnp.float32), panel_cols.astype(jnp.float32), precision=precise, preferred_element_type=jnp.float32)
        pushed = pushed + jnp.dot(trailing.T.astype(jnp.float32), panel_cols.astype(jnp.float32), precision=precise, preferred_element_type=jnp.float32)
        panel_sums = result[end_row:, first_row:end_row] - pushed
        solved = jax.scipy.linalg.solve_triangular(pivot_block, panel_sums.T, trans=1, lower=True).T
        diag_target = result[first_row:end_row, first_row:end_row] - jnp.tril(jnp.dot(solved.T.astype(jnp.float32), panel_cols.astype(jnp.float32), precision=precise, preferred_element_type=jnp.float32))
        diag_adjoint = cholesky_adjoint(pivot_block, diag_target)
        result = result.at[end_row:, first_row:end_row].set(solved)
        result = result.at[first_row:end_row, first_row:end_row].set(diag_adjoint)
    return result.reshape(BLOCKS_DOWN, GRID_ROWS, BLOCK, BLOCKS_ACROSS, GRID_COLS, BLOCK)
```

```python
import jax
import jax.numpy as jnp
from jax import lax
from jax.experimental import pallas as pl
from jax.experimental.pallas import tpu as pltpu
from jax.sharding import PartitionSpec as P

F32, BF16 = jnp.float32, jnp.bfloat16
MESH = pl.DeviceIdType.MESH
precise = lax.Precision.HIGHEST


def up(v):
    return lax.rem(v + 1, 4)


def down(v):
    return lax.rem(v + 3, 4)


def across_from(v):
    return lax.rem(v + 2, 4)


def split(value):
    high = value.astype(BF16)
    return high, (value - high.astype(F32)).astype(BF16)


def dot(left, right):
    return jnp.dot(left, right, preferred_element_type=F32)


def dot3(left, right):
    (left_high, left_low), (right_high, right_low) = left, right
    return dot(left_high, right_high) + (dot(left_high, right_low) + dot(left_low, right_high))


def exact(left, right):
    return jnp.dot(left, right, precision=precise, preferred_element_type=F32)


def iotas(shape):
    return (
        lax.broadcasted_iota(jnp.int32, shape, 0),
        lax.broadcasted_iota(jnp.int32, shape, 1),
    )


def lower(matrix):
    row, col = iotas(matrix.shape)
    return jnp.where(row >= col, matrix, 0.0)


def halve_diag(matrix):
    row, col = iotas(matrix.shape)
    return jnp.where(row > col, matrix, jnp.where(row == col, 0.5 * matrix, 0.0))


def inverses(blocks):
    row, col = iotas(blocks[0].shape)
    found = [jnp.where(row == col, 1.0 / jnp.where(row == col, q, 1.0), 0.0) for q in blocks]
    size = 1
    while size < blocks[0].shape[0]:
        here = jnp.logical_and(row // (2 * size) == col // (2 * size), row // size > col // size)
        left = [exact(x, jnp.where(here, q, 0.0)) for x, q in zip(found, blocks)]
        found = [x - exact(y, x) for x, y in zip(found, left)]
        size *= 2
    return found


def diag_step(pivot, inverse, target):
    inner = halve_diag(exact(pivot.T, target))
    return halve_diag(exact(exact(inverse.T, inner), inverse))


def sweep_kernel(
    panel,
    adj,
    out,
    s_ref,
    crow,
    ccol,
    ct,
    sw,
    cc,
    oacc,
    macc,
    mate_in,
    yopp,
    ynbr,
    moved,
    opp1,
    nbr1,
    opp2,
    nbr2,
    agath,
    apiece,
    qbuf,
    qinv,
    tbuf,
    trecv,
    tslice,
    tall1,
    tall0,
    rblk,
    rsend,
    done,
    a01,
    local_sem,
    scat_s,
    scat_r,
    ag1,
    ag2,
    chain_s,
    chain_r,
    q_s,
    q_r,
    ring,
    mate_sem,
    moved_sem,
    ga_s,
    ga_r,
    t_s,
    t_r,
    root_s,
    root_r,
    blk_sem,
):
    r, c = lax.axis_index("row"), lax.axis_index("col")
    y, core = lax.div(r, 2), lax.rem(r, 2)
    z, x = lax.div(c, 4), lax.rem(c, 4)
    place = ((x, z), (z, x))
    home = lax.rem(c, 8)
    home_y, home_core = lax.div(home, 2), lax.rem(home, 2)
    group = lax.div(c, 8)
    mate = (y * 2 + 1 - core, c)
    target = (home, 4 * y + 2 * group + core)
    giver = (2 * z + lax.rem(x, 2), r + 8 * lax.div(x, 2))
    pending = []

    def piece(p, first, second):
        return second * 4 + first if p == 0 else first * 4 + second

    def member(p, first, second):
        return (r, piece(p, first, second))

    def send(src, dst, ss, rs, device):
        copy = pltpu.make_async_remote_copy(
            src_ref=src, dst_ref=dst, send_sem=ss, recv_sem=rs, device_id=device, device_id_type=MESH
        )
        copy.start()
        return copy

    def post(*args):
        pending.append(send(*args))

    def arrived(dst, rs):
        pltpu.make_async_remote_copy(
            src_ref=dst, dst_ref=dst, send_sem=rs, recv_sem=rs, device_id=mate, device_id_type=MESH
        ).wait_recv()

    def left(src, ss):
        pltpu.make_async_remote_copy(
            src_ref=src, dst_ref=src, send_sem=ss, recv_sem=ss, device_id=mate, device_id_type=MESH
        ).wait_send()

    load = pltpu.make_async_copy(adj, s_ref, local_sem.at[0])
    load.start()

    barrier = pltpu.get_barrier_semaphore()

    def greet(device):
        pl.semaphore_signal(barrier, inc=1, device_id=device, device_id_type=MESH)

    for step in range(1, 16):
        greet((r, lax.rem(c + step, 16)))
    for step in range(1, 8):
        greet((lax.rem(r + step, 8), c))
    away = jnp.logical_or(target[0] != r, target[1] != c)
    from_away = jnp.logical_or(giver[0] != r, giver[1] != c)
    is_root = jnp.logical_and(r == 0, c == 0)
    owes_root = jnp.logical_and(r > 0, c == 1)

    @pl.when(from_away)
    def _():
        greet(giver)

    @pl.when(is_root)
    def _():
        for step in range(1, 8):
            greet((step, 1))

    pl.semaphore_wait(barrier, 22 + jnp.where(away, 1, 0) + jnp.where(owes_root, 1, 0))

    order = (10, 11, 14, 15, 6, 7, 8, 9, 12, 13, 2, 3, 5, 4, 1, 0)
    for p in range(2):

        @pl.when(c == p)
        def _():
            for k in order:
                if k != p:
                    send(panel.at[k], crow.at[p, k], scat_s.at[k], scat_r.at[p], (r, k))
            own = pltpu.make_async_copy(panel.at[p], crow.at[p, p], local_sem.at[1])
            own.start()
            own.wait()

    def halves(ref, half):
        return ref.at[pl.ds(64 * half, 64)]

    def gather_second(p, q, first):
        f, s = place[p]
        held = crow.at[p, piece(p, first, s)]
        post(held, held, ag2.at[0, p, q, 0], ag2.at[1, p, q, 0], member(p, f, up(s)))
        post(held, held, ag2.at[0, p, q, 1], ag2.at[1, p, q, 1], member(p, f, down(s)))

    for p in range(2):
        f, s = place[p]
        held = crow.at[p, piece(p, f, s)]

        @pl.when(c != p)
        def _():
            arrived(crow.at[p, c], scat_r.at[p])

        post(held, held, ag1.at[0, p, 0], ag1.at[1, p, 0], member(p, up(f), s))
        post(held, held, ag1.at[0, p, 1], ag1.at[1, p, 1], member(p, down(f), s))
        gather_second(p, 0, f)
    for p in range(2):
        f, s = place[p]
        held = crow.at[p, piece(p, down(f), s)]
        arrived(held, ag1.at[1, p, 0])
        part = halves(held, 0)
        post(part, part, ag1.at[0, p, 2], ag1.at[1, p, 2], member(p, up(f), s))
        gather_second(p, 1, down(f))
        held = crow.at[p, piece(p, up(f), s)]
        arrived(held, ag1.at[1, p, 1])
        part = halves(held, 1)
        post(part, part, ag1.at[0, p, 3], ag1.at[1, p, 3], member(p, down(f), s))
        gather_second(p, 2, up(f))
    for p in range(2):
        f, s = place[p]
        held = crow.at[p, piece(p, across_from(f), s)]
        arrived(halves(held, 0), ag1.at[1, p, 2])
        arrived(halves(held, 1), ag1.at[1, p, 3])
        gather_second(p, 3, across_from(f))
    for q in range(4):
        for p in range(2):
            f, s = place[p]
            first = (f, down(f), up(f), across_from(f))[q]
            held = crow.at[p, piece(p, first, down(s))]
            arrived(held, ag2.at[1, p, q, 0])
            part = halves(held, 0)
            post(part, part, ag2.at[0, p, q, 2], ag2.at[1, p, q, 2], member(p, f, up(s)))
            held = crow.at[p, piece(p, first, up(s))]
            arrived(held, ag2.at[1, p, q, 1])
            part = halves(held, 1)
            post(part, part, ag2.at[0, p, q, 3], ag2.at[1, p, q, 3], member(p, f, down(s)))
    for q in range(4):
        for p in range(2):
            f, s = place[p]
            first = (f, down(f), up(f), across_from(f))[q]
            held = crow.at[p, piece(p, first, across_from(s))]
            arrived(halves(held, 0), ag2.at[1, p, q, 2])
            arrived(halves(held, 1), ag2.at[1, p, q, 3])

    load.wait()

    in_line = core == home_core
    is_home = jnp.logical_and(in_line, y == home_y)
    relays = jnp.logical_and(in_line, y != home_y)
    next_y = (up(y), down(y))
    gap = (lax.rem(y - home_y + 4, 4), lax.rem(home_y - y + 4, 4))

    def home_pieces(p, b):
        return crow.at[p, pl.ds(4 * b + 2 * group, 2)]

    chunks = [(p, b) for b in range(4) for p in range(2)]

    @pl.when(is_home)
    def _():
        for p, b in chunks:
            src = home_pieces(p, b)
            send(src, ccol.at[p, b], chain_s.at[p, b, 0], chain_r.at[p, b], (next_y[p] * 2 + core, c))
            send(src, ccol.at[p, b], chain_s.at[p, b, 1], chain_r.at[p, b], mate)
            pltpu.make_async_copy(src, ccol.at[p, b], local_sem.at[2 + p * 4 + b]).start()

    def relay(p, b):
        @pl.when(relays)
        def _():
            held = ccol.at[p, b]
            arrived(held, chain_r.at[p, b])

            @pl.when(gap[p] < 3)
            def _():
                send(held, held, chain_s.at[p, b, 0], chain_r.at[p, b], (next_y[p] * 2 + core, c))

            send(held, held, chain_s.at[p, b, 1], chain_r.at[p, b], mate)

    pivots = ((0, 0, 0), (1, 0, 1), (2, 1, 1))

    for slot, p, holder in pivots:

        @pl.when(r == holder)
        def _():
            src = crow.at[p, pl.ds(0, 2)]
            send(src, qbuf.at[slot], q_s.at[slot, 0], q_r.at[slot], (2 + holder, c))
            send(src, qbuf.at[slot], q_s.at[slot, 1], q_r.at[slot], (6 + holder, c))
            send(src, qbuf.at[slot], q_s.at[slot, 2], q_r.at[slot], (4 + holder, c))
            send(src, qbuf.at[slot], q_s.at[slot, 3], q_r.at[slot], mate)
            own = pltpu.make_async_copy(src, qbuf.at[slot], local_sem.at[1])
            own.start()
            own.wait()

    def adjoint_block(a, b):
        return jnp.concatenate(
            [s_ref[pl.ds(a * 2048 + 2 * b + h, 256, stride=8), :] for h in range(2)], axis=1
        )

    at_11 = jnp.logical_and(r == 1, c == 1)
    at_10 = jnp.logical_and(r == 1, c == 0)

    @pl.when(at_11)
    def _():
        rsend[...] = adjoint_block(0, 0)
        send(rsend, rblk.at[0], blk_sem.at[0], blk_sem.at[2], (0, 0))

    @pl.when(at_10)
    def _():
        rsend[...] = adjoint_block(0, 0)
        send(rsend, rblk.at[1], blk_sem.at[1], blk_sem.at[3], (0, 0))

    row_iota, col_iota = iotas((256, 256))

    def active(a, b):
        i, j = 8 * a + r, 16 * b + c
        return jnp.logical_and(j >= 2, j <= i)

    macc[...] = jnp.zeros_like(macc)

    def mirrored(a):
        for p in range(2):
            for half in range(2):
                high, low = split(crow[p, 2 * a + half])
                lanes = pl.ds(128 * half, 128)
                ct[0, pl.ds(256 * p, 256), lanes] = high.T
                ct[1, pl.ds(256 * p, 256), lanes] = low.T

        def per_block(b, carry):
            @pl.when(active(a, b))
            def _():
                shift = 256 * (8 * a + r - 16 * b - c)
                block = jnp.where(row_iota + shift >= col_iota, adjoint_block(a, b), 0.0)
                high, low = split(block)
                sw[0, a, b] = high
                sw[1, a, b] = low
                total = dot3((ct[0], ct[1]), (high, low))
                macc[b, 0] += total[:, :128]
                macc[b, 1] += total[:, 128:]

            return carry

        lax.fori_loop(0, 4, per_block, 0)

    for step, (p, b) in enumerate(chunks):
        mirrored(step)
        relay(p, b)

    for b in range(4):
        post(
            macc.at[b, 1 - core], mate_in.at[b], mate_sem.at[0, b], mate_sem.at[1, b], mate
        )

    @pl.when(is_home)
    def _():
        for p, b in chunks:
            pltpu.make_async_copy(home_pieces(p, b), ccol.at[p, b], local_sem.at[2 + p * 4 + b]).wait()

    @pl.when(jnp.logical_not(in_line))
    def _():
        for p, b in chunks:
            arrived(ccol.at[p, b], chain_r.at[p, b])

    def ready_columns(b, carry):
        for p in range(2):
            for half in range(2):
                high, low = split(ccol[p, b, half])
                rows, lanes = pl.ds(128 * half, 128), pl.ds(256 * p, 256)
                cc[0, b, rows, lanes] = high
                cc[1, b, rows, lanes] = low
        return carry

    lax.fori_loop(0, 4, ready_columns, 0)

    oacc[...] = jnp.zeros_like(oacc)

    def direct(a, carry):
        for p in range(2):

            @pl.when(c == p)
            def _():
                block = adjoint_block(a, 0)
                oacc[p, 2 * a] = -block[:128]
                oacc[p, 2 * a + 1] = -block[128:]

        def per_block(b, inner):
            @pl.when(active(a, b))
            def _():
                total = dot3((sw[0, a, b], sw[1, a, b]), (cc[0, b], cc[1, b]))
                for p in range(2):
                    for half in range(2):
                        oacc[p, 2 * a + half] += total[128 * half : 128 * half + 128, 256 * p : 256 * p + 256]

            return inner

        lax.fori_loop(0, 4, per_block, 0)
        return carry

    lax.fori_loop(0, 8, direct, 0)

    def ring_open(slot, held, pos, device, rows, opp, nbr):
        def part(ref, half):
            return ref.at[pl.ds(rows * half, rows)]

        def go(src, dst, n, where):
            post(src, dst, ring.at[0, slot, n], ring.at[1, slot, n], device(where))

        far = held(across_from(pos))
        go(part(far, 0), opp.at[0], 0, down(pos))
        go(part(far, 1), opp.at[1], 1, up(pos))
        go(part(held(down(pos)), 1), part(nbr.at[0], 1), 2, down(pos))
        go(part(held(up(pos)), 0), part(nbr.at[1], 0), 3, up(pos))

    def ring_pass(slot, held, pos, device, rows, opp, nbr):
        def part(ref, half):
            return ref.at[pl.ds(rows * half, rows)]

        def go(src, dst, n, where):
            post(src, dst, ring.at[0, slot, n], ring.at[1, slot, n], device(where))

        arrived(opp.at[0], ring.at[1, slot, 0])
        mine = part(held(down(pos)), 0)
        mine[...] = mine[...] + opp[0]
        go(mine, part(nbr.at[0], 0), 4, down(pos))
        arrived(opp.at[1], ring.at[1, slot, 1])
        mine = part(held(up(pos)), 1)
        mine[...] = mine[...] + opp[1]
        go(mine, part(nbr.at[1], 1), 5, up(pos))

    def ring_close(slot, held, pos, device, rows, opp, nbr):
        def part(ref, half):
            return ref.at[pl.ds(rows * half, rows)]

        arrived(part(nbr.at[0], 1), ring.at[1, slot, 2])
        arrived(part(nbr.at[0], 0), ring.at[1, slot, 4])
        arrived(part(nbr.at[1], 0), ring.at[1, slot, 3])
        arrived(part(nbr.at[1], 1), ring.at[1, slot, 5])
        mine = held(pos)
        mine[...] = mine[...] + (nbr[0] + nbr[1])

    def first_ring(p, j):
        f, s = place[p]
        return (
            4 * p + j,
            lambda t: oacc.at[p, piece(p, j, t)],
            s,
            lambda t: member(p, f, t),
            64,
            opp1.at[p, j],
            nbr1.at[p, j],
        )

    def second_ring(p):
        f, s = place[p]
        return (
            8 + p,
            lambda t: oacc.at[p, piece(p, t, s)],
            f,
            lambda t: member(p, t, s),
            64,
            opp2.at[p],
            nbr2.at[p],
        )

    column_ring = (
        10,
        lambda t: macc.at[t, core],
        y,
        lambda t: (t * 2 + core, c),
        256,
        yopp,
        ynbr,
    )
    rings = [first_ring(p, j) for j in range(4) for p in range(2)]
    for spec in rings:
        ring_open(*spec)

    for b in range(4):
        arrived(mate_in.at[b], mate_sem.at[1, b])
    for b in range(4):
        mine = macc.at[b, core]
        mine[...] = mine[...] + mate_in[b]
    ring_open(*column_ring)

    for spec in rings:
        ring_pass(*spec)
    ring_pass(*column_ring)

    for slot, p, holder in pivots:

        @pl.when(r != holder)
        def _():
            arrived(qbuf.at[slot], q_r.at[slot])

            @pl.when(core == holder)
            def _():
                send(qbuf.at[slot], qbuf.at[slot], q_s.at[slot, 3], q_r.at[slot], mate)

    def pivot(slot):
        return jnp.concatenate([qbuf[slot, 0], qbuf[slot, 1]], axis=0)

    inverse_0, inverse_1 = inverses([pivot(0), pivot(2)])
    qinv[0] = inverse_0
    qinv[1] = inverse_1

    for spec in rings:
        ring_close(*spec)
    for p in range(2):
        ring_open(*second_ring(p))
    ring_close(*column_ring)

    @pl.when(away)
    def _():
        send(macc.at[y, core], moved, moved_sem.at[0], moved_sem.at[1], target)

    @pl.when(jnp.logical_not(away))
    def _():
        moved[...] = macc[y, core]

    for p in range(2):
        ring_pass(*second_ring(p))
    for p in range(2):
        ring_close(*second_ring(p))

    @pl.when(from_away)
    def _():
        arrived(moved, moved_sem.at[1])

    keep = jnp.where(jnp.logical_and(c < 2, r < 2), 0.0, -1.0)
    extra = moved[...].T
    sums_1 = (oacc[1, c] + extra[:, 256:]) * keep
    sums_0 = (oacc[0, c] + extra[:, :256]) * keep
    solved_1 = exact(sums_1, qinv[1])
    apiece[1] = solved_1

    def hand_in(p):
        @pl.when(c != p)
        def _():
            send(apiece.at[p], agath.at[c], ga_s.at[p], ga_r.at[c], (r, p))

    hand_in(1)
    solved_0 = exact(sums_0 - exact(solved_1, pivot(1)), qinv[0])
    apiece[0] = solved_0
    hand_in(0)

    @pl.when(c < 2)
    def _():
        for p in range(2):

            @pl.when(c == p)
            def _():
                agath[p] = apiece[p]

                for k in range(16):
                    if k != p:
                        arrived(agath.at[k], ga_r.at[k])

        def gathered(k, total):
            high, low = split(agath[k])
            sides = (high.T, low.T)
            first = dot3(sides, split(crow[c, k]))
            second = dot3(sides, split(crow[0, k]))
            return total[0] + first, total[1] + second

        zero = jnp.zeros((256, 256), F32)
        total = lax.fori_loop(0, 16, gathered, (zero, zero))
        for t in range(8):
            for n in range(2):
                tbuf[t, n] = total[n][32 * t : 32 * t + 32]
        for step in range(1, 8):
            to = lax.rem(r + step, 8)
            send(tbuf.at[to], trecv.at[step], t_s.at[step], t_r.at[step], (to, c))
        result = tbuf[r]
        for step in range(1, 8):
            arrived(trecv.at[step], t_r.at[step])
            result = result + trecv[step]
        tslice[...] = result

        @pl.when(c == 1)
        def _():
            send(tslice, tall1.at[r], root_s.at[0], root_r.at[0, r], (0, 0))

            @pl.when(r != 1)
            def _():
                send(tslice, tall1.at[r], root_s.at[1], root_r.at[0, r], (1, 1))

        @pl.when(jnp.logical_and(c == 0, r != 0))
        def _():
            send(tslice.at[0], tall0.at[r], root_s.at[0], root_r.at[1, r], (0, 0))

    def flat(parts):
        return jnp.concatenate(parts, axis=0)

    @pl.when(at_11)
    def _():
        tall1[1] = tslice[...]
        for t in range(8):
            if t != 1:
                arrived(tall1.at[t], root_r.at[0, t])
        sums = flat([tall1[t, 0] for t in range(8)])
        done[...] = diag_step(pivot(2), qinv[1], lower(adjoint_block(0, 0) - sums))

    @pl.when(is_root)
    def _():
        tall0[0] = tslice[0]
        for t in range(8):
            arrived(tall1.at[t], root_r.at[0, t])
        arrived(rblk.at[0], blk_sem.at[2])
        arrived(rblk.at[1], blk_sem.at[3])
        sums = flat([tall1[t, 0] for t in range(8)])
        diag_1 = diag_step(pivot(2), qinv[1], lower(rblk[0] - sums))
        cross = flat([tall1[t, 1] for t in range(8)])
        link = pivot(1)
        rows_1 = exact(rblk[1] - cross - exact(diag_1 + diag_1.T, link), qinv[0])
        rsend[...] = rows_1
        send(rsend, a01, blk_sem.at[4], blk_sem.at[5], (1, 0))
        for t in range(1, 8):
            arrived(tall0.at[t], root_r.at[1, t])
        sums = flat([tall0[t] for t in range(8)]) + exact(rows_1.T, link)
        done[...] = diag_step(pivot(0), qinv[0], lower(adjoint_block(0, 0) - sums))
        left(rsend, blk_sem.at[4])

    @pl.when(at_10)
    def _():
        arrived(a01, blk_sem.at[5])
        done[...] = a01[...]

    @pl.when(c < 2)
    def _():
        def write(k, carry):
            value = agath[k]
            for h in range(2):
                out[pl.ds(256 * k + h, 128, stride=2), :] = value[:, 128 * h : 128 * h + 128]
            return carry

        lax.fori_loop(0, 16, write, 0)

        @pl.when(jnp.logical_and(r < 2, jnp.logical_or(r == 1, c == 0)))
        def _():
            value = done[...]
            for h in range(2):
                out[pl.ds(h, 256, stride=2), :] = value[:, 128 * h : 128 * h + 128]

    @pl.when(c >= 2)
    def _():
        out[...] = jnp.zeros_like(out)

    for copy in pending:
        copy.wait_send()
    for p in range(2):

        @pl.when(c == p)
        def _():
            for k in range(16):
                if k != p:
                    left(panel.at[k], scat_s.at[k])

        @pl.when(c != p)
        def _():
            left(apiece.at[p], ga_s.at[p])

    for p, b in chunks:

        @pl.when(in_line)
        def _():
            left(ccol.at[p, b], chain_s.at[p, b, 1])

            @pl.when(gap[p] < 3)
            def _():
                left(ccol.at[p, b], chain_s.at[p, b, 0])

    for slot, p, holder in pivots:

        @pl.when(core == holder)
        def _():
            left(qbuf.at[slot], q_s.at[slot, 3])

        @pl.when(r == holder)
        def _():
            for n in range(3):
                left(qbuf.at[slot], q_s.at[slot, n])

    @pl.when(at_11)
    def _():
        left(rsend, blk_sem.at[0])

    @pl.when(at_10)
    def _():
        left(rsend, blk_sem.at[1])

    @pl.when(away)
    def _():
        left(moved, moved_sem.at[0])

    @pl.when(c < 2)
    def _():
        for step in range(1, 8):
            left(trecv.at[step], t_s.at[step])

        @pl.when(c == 1)
        def _():
            left(tslice, root_s.at[0])

            @pl.when(r != 1)
            def _():
                left(tslice, root_s.at[1])

        @pl.when(jnp.logical_and(c == 0, r != 0))
        def _():
            left(tslice.at[0], root_s.at[0])


def sweep(panel, adj):
    vmem = pltpu.VMEM
    dma = pltpu.SemaphoreType.DMA
    return pl.pallas_call(
        sweep_kernel,
        out_shape=jax.ShapeDtypeStruct((4096, 128), F32),
        in_specs=[pl.BlockSpec(memory_space=pl.ANY)] * 2,
        out_specs=pl.BlockSpec(memory_space=pltpu.VMEM),
        scratch_shapes=[
            vmem((16384, 128), F32),
            vmem((2, 16, 128, 256), F32),
            vmem((2, 4, 2, 128, 256), F32),
            vmem((2, 512, 256), BF16),
            vmem((2, 8, 4, 256, 256), BF16),
            vmem((2, 4, 256, 512), BF16),
            vmem((2, 16, 128, 256), F32),
            vmem((4, 2, 512, 128), F32),
            vmem((4, 512, 128), F32),
            vmem((2, 256, 128), F32),
            vmem((2, 512, 128), F32),
            vmem((512, 128), F32),
            vmem((2, 4, 2, 64, 256), F32),
            vmem((2, 4, 2, 128, 256), F32),
            vmem((2, 2, 64, 256), F32),
            vmem((2, 2, 128, 256), F32),
            vmem((16, 128, 256), F32),
            vmem((2, 128, 256), F32),
            vmem((3, 2, 128, 256), F32),
            vmem((2, 256, 256), F32),
            vmem((8, 2, 32, 256), F32),
            vmem((8, 2, 32, 256), F32),
            vmem((2, 32, 256), F32),
            vmem((8, 2, 32, 256), F32),
            vmem((8, 32, 256), F32),
            vmem((2, 256, 256), F32),
            vmem((256, 256), F32),
            vmem((256, 256), F32),
            vmem((256, 256), F32),
            dma((10,)),
            dma((16,)),
            dma((2,)),
            dma((2, 2, 4)),
            dma((2, 2, 4, 4)),
            dma((2, 4, 2)),
            dma((2, 4)),
            dma((3, 4)),
            dma((3,)),
            dma((2, 11, 6)),
            dma((2, 4)),
            dma((2,)),
            dma((2,)),
            dma((16,)),
            dma((8,)),
            dma((8,)),
            dma((2,)),
            dma((2, 8)),
            dma((6,)),
        ],
        compiler_params=pltpu.CompilerParams(
            collective_id=0, has_side_effects=True, vmem_limit_bytes=60 * 2**20
        ),
        name="sweep",
    )(panel, adj)


def merge_kernel(adj, panel, out):
    r, c = lax.axis_index("row"), lax.axis_index("col")
    a = pl.program_id(0)
    shape = (256, 8, 128)
    slot = lax.broadcasted_iota(jnp.int32, (1, 8, 128), 1)
    lane = lax.broadcasted_iota(jnp.int32, (1, 8, 128), 2)
    col = (16 * (slot // 2) + c) * 256 + lax.rem(slot, 2) * 128 + lane
    row = (8 * a + r) * 256 + lax.broadcasted_iota(jnp.int32, shape, 0)
    value = jnp.where(row >= col, adj[...].reshape(shape), 0.0)
    out[...] = value.reshape(2048, 128)

    @pl.when(c < 2)
    def _():
        for h in range(2):
            out[pl.ds(h, 256, stride=8), :] = panel[pl.ds(h, 256, stride=2), :]


def merge(adj, panel):
    return pl.pallas_call(
        merge_kernel,
        grid=(8,),
        out_shape=jax.ShapeDtypeStruct((16384, 128), F32),
        in_specs=[
            pl.BlockSpec((2048, 128), lambda a: (a, 0)),
            pl.BlockSpec((512, 128), lambda a: (a, 0)),
        ],
        out_specs=pl.BlockSpec((2048, 128), lambda a: (a, 0)),
        compiler_params=pltpu.CompilerParams(vmem_limit_bytes=32 * 2**20),
        name="merge",
    )(adj, panel)


def shards(factor, adjoint):
    panel = factor[:, 0, :, 0, 0, :].reshape(16, 128, 256)
    adj = adjoint.reshape(16384, 128)
    solved = sweep(panel, adj)
    return merge(adj, solved).reshape(adjoint.shape)


def solution(mesh):
    spec = P(None, "row", None, None, "col", None)
    return jax.shard_map(
        shards,
        mesh=mesh,
        in_specs=(spec, spec),
        out_specs=spec,
        check_vma=False,
    )
```

```python
import jax
import jax.numpy as jnp
from jax import lax
from jax.experimental import pallas as pl
from jax.experimental.pallas import tpu as pltpu
from jax.sharding import PartitionSpec as P

F32, BF16 = jnp.float32, jnp.bfloat16
MESH = pl.DeviceIdType.MESH
precise = lax.Precision.HIGHEST


def up(v):
    return lax.rem(v + 1, 4)


def down(v):
    return lax.rem(v + 3, 4)


def across_from(v):
    return lax.rem(v + 2, 4)


def split(value):
    high = value.astype(BF16)
    return high, (value - high.astype(F32)).astype(BF16)


def dot(left, right):
    return jnp.dot(left, right, preferred_element_type=F32)


def dot3(left, right):
    (left_high, left_low), (right_high, right_low) = left, right
    return dot(left_high, right_high) + (dot(left_high, right_low) + dot(left_low, right_high))


def exact(left, right):
    return jnp.dot(left, right, precision=precise, preferred_element_type=F32)


def iotas(shape):
    return (
        lax.broadcasted_iota(jnp.int32, shape, 0),
        lax.broadcasted_iota(jnp.int32, shape, 1),
    )


def lower(matrix):
    row, col = iotas(matrix.shape)
    return jnp.where(row >= col, matrix, 0.0)


def halve_diag(matrix):
    row, col = iotas(matrix.shape)
    return jnp.where(row > col, matrix, jnp.where(row == col, 0.5 * matrix, 0.0))


def inverses(blocks):
    row, col = iotas(blocks[0].shape)
    found = [jnp.where(row == col, 1.0 / jnp.where(row == col, q, 1.0), 0.0) for q in blocks]
    size = 1
    while size < blocks[0].shape[0]:
        here = jnp.logical_and(row // (2 * size) == col // (2 * size), row // size > col // size)
        left = [exact(x, jnp.where(here, q, 0.0)) for x, q in zip(found, blocks)]
        found = [x - exact(y, x) for x, y in zip(found, left)]
        size *= 2
    return found


def diag_step(pivot, inverse, target):
    inner = halve_diag(exact(pivot.T, target))
    return halve_diag(exact(exact(inverse.T, inner), inverse))


def sweep_kernel(
    factor,
    adj,
    out,
    s_ref,
    panel,
    crow,
    ccol,
    ct,
    sw,
    cc,
    oacc,
    macc,
    mate_in,
    yopp,
    ynbr,
    moved,
    opp1,
    nbr1,
    opp2,
    nbr2,
    agath,
    apiece,
    qbuf,
    qinv,
    tpart,
    tin1,
    tsum,
    tin2,
    tslice,
    tin3,
    tall,
    rblk,
    rsend,
    done,
    a01,
    local_sem,
    scat_s,
    scat_r,
    ag1,
    ag2,
    chain_s,
    chain_r,
    q_s,
    q_r,
    ring,
    mate_sem,
    moved_sem,
    ga_s,
    ga_r,
    t1,
    t2,
    t3,
    troot,
    blk_sem,
):
    r, c = lax.axis_index("row"), lax.axis_index("col")
    y, core = lax.div(r, 2), lax.rem(r, 2)
    z, x = lax.div(c, 4), lax.rem(c, 4)
    place = ((x, z), (z, x))
    home = lax.rem(c, 8)
    home_y, home_core = lax.div(home, 2), lax.rem(home, 2)
    group = lax.div(c, 8)
    mate = (y * 2 + 1 - core, c)
    target = (home, 4 * y + 2 * group + core)
    giver = (2 * z + lax.rem(x, 2), r + 8 * lax.div(x, 2))
    pending = []

    def piece(p, first, second):
        return second * 4 + first if p == 0 else first * 4 + second

    def member(p, first, second):
        return (r, piece(p, first, second))

    def send(src, dst, ss, rs, device):
        copy = pltpu.make_async_remote_copy(
            src_ref=src, dst_ref=dst, send_sem=ss, recv_sem=rs, device_id=device, device_id_type=MESH
        )
        copy.start()
        return copy

    def post(*args):
        pending.append(send(*args))

    def arrived(dst, rs):
        pltpu.make_async_remote_copy(
            src_ref=dst, dst_ref=dst, send_sem=rs, recv_sem=rs, device_id=mate, device_id_type=MESH
        ).wait_recv()

    def left(src, ss):
        pltpu.make_async_remote_copy(
            src_ref=src, dst_ref=src, send_sem=ss, recv_sem=ss, device_id=mate, device_id_type=MESH
        ).wait_send()

    holds_panel = c < 2
    load = pltpu.make_async_copy(adj, s_ref, local_sem.at[0])

    @pl.when(holds_panel)
    def _():
        pltpu.make_async_copy(factor, s_ref, local_sem.at[1]).start()

    barrier = pltpu.get_barrier_semaphore()

    def greet(device):
        pl.semaphore_signal(barrier, inc=1, device_id=device, device_id_type=MESH)

    for step in range(1, 16):
        greet((r, lax.rem(c + step, 16)))
    for step in range(1, 8):
        greet((lax.rem(r + step, 8), c))
    away = jnp.logical_or(target[0] != r, target[1] != c)
    from_away = jnp.logical_or(giver[0] != r, giver[1] != c)
    is_root = jnp.logical_and(r == 0, c == 0)
    owes_root = jnp.logical_and(r > 0, jnp.logical_and(c > 0, c < 4))
    at_11 = jnp.logical_and(r == 1, c == 1)
    at_10 = jnp.logical_and(r == 1, c == 0)

    @pl.when(from_away)
    def _():
        greet(giver)

    @pl.when(is_root)
    def _():
        for step in range(1, 8):
            for other in range(1, 4):
                greet((step, other))

    @pl.when(at_11)
    def _():
        greet((0, 0))

    @pl.when(holds_panel)
    def _():
        pltpu.make_async_copy(factor, s_ref, local_sem.at[1]).wait()

        def take(k, carry):
            for h in range(2):
                panel[k, :, pl.ds(128 * h, 128)] = s_ref[pl.ds(k * 1024 + h, 128, stride=8), :]
            return carry

        lax.fori_loop(0, 16, take, 0)

    load.start()
    pl.semaphore_wait(
        barrier,
        22 + jnp.where(away, 1, 0) + jnp.where(owes_root, 1, 0) + jnp.where(is_root, 1, 0),
    )

    order = (10, 11, 14, 15, 6, 7, 8, 9, 12, 13, 2, 3, 5, 4, 1, 0)
    for p in range(2):

        @pl.when(c == p)
        def _():
            for k in order:
                if k != p:
                    send(panel.at[k], crow.at[p, k], scat_s.at[k], scat_r.at[p], (r, k))
            own = pltpu.make_async_copy(panel.at[p], crow.at[p, p], local_sem.at[1])
            own.start()
            own.wait()

    def halves(ref, half):
        return ref.at[pl.ds(64 * half, 64)]

    def gather_second(p, q, first):
        f, s = place[p]
        held = crow.at[p, piece(p, first, s)]
        post(held, held, ag2.at[0, p, q, 0], ag2.at[1, p, q, 0], member(p, f, up(s)))
        post(held, held, ag2.at[0, p, q, 1], ag2.at[1, p, q, 1], member(p, f, down(s)))

    for p in range(2):
        f, s = place[p]
        held = crow.at[p, piece(p, f, s)]

        @pl.when(c != p)
        def _():
            arrived(crow.at[p, c], scat_r.at[p])

        post(held, held, ag1.at[0, p, 0], ag1.at[1, p, 0], member(p, up(f), s))
        post(held, held, ag1.at[0, p, 1], ag1.at[1, p, 1], member(p, down(f), s))
        gather_second(p, 0, f)
    for p in range(2):
        f, s = place[p]
        held = crow.at[p, piece(p, down(f), s)]
        arrived(held, ag1.at[1, p, 0])
        part = halves(held, 0)
        post(part, part, ag1.at[0, p, 2], ag1.at[1, p, 2], member(p, up(f), s))
        gather_second(p, 1, down(f))
        held = crow.at[p, piece(p, up(f), s)]
        arrived(held, ag1.at[1, p, 1])
        part = halves(held, 1)
        post(part, part, ag1.at[0, p, 3], ag1.at[1, p, 3], member(p, down(f), s))
        gather_second(p, 2, up(f))
    for p in range(2):
        f, s = place[p]
        held = crow.at[p, piece(p, across_from(f), s)]
        arrived(halves(held, 0), ag1.at[1, p, 2])
        arrived(halves(held, 1), ag1.at[1, p, 3])
        gather_second(p, 3, across_from(f))
    for q in range(4):
        for p in range(2):
            f, s = place[p]
            first = (f, down(f), up(f), across_from(f))[q]
            held = crow.at[p, piece(p, first, down(s))]
            arrived(held, ag2.at[1, p, q, 0])
            part = halves(held, 0)
            post(part, part, ag2.at[0, p, q, 2], ag2.at[1, p, q, 2], member(p, f, up(s)))
            held = crow.at[p, piece(p, first, up(s))]
            arrived(held, ag2.at[1, p, q, 1])
            part = halves(held, 1)
            post(part, part, ag2.at[0, p, q, 3], ag2.at[1, p, q, 3], member(p, f, down(s)))
    for q in range(4):
        for p in range(2):
            f, s = place[p]
            first = (f, down(f), up(f), across_from(f))[q]
            held = crow.at[p, piece(p, first, across_from(s))]
            arrived(halves(held, 0), ag2.at[1, p, q, 2])
            arrived(halves(held, 1), ag2.at[1, p, q, 3])

    load.wait()

    in_line = core == home_core
    is_home = jnp.logical_and(in_line, y == home_y)
    relays = jnp.logical_and(in_line, y != home_y)
    next_y = (up(y), down(y))
    gap = (lax.rem(y - home_y + 4, 4), lax.rem(home_y - y + 4, 4))

    def home_pieces(p, b):
        return crow.at[p, pl.ds(4 * b + 2 * group, 2)]

    chunks = [(p, b) for b in range(4) for p in range(2)]

    @pl.when(is_home)
    def _():
        for p, b in chunks:
            src = home_pieces(p, b)
            send(src, ccol.at[p, b], chain_s.at[p, b, 0], chain_r.at[p, b], (next_y[p] * 2 + core, c))
            send(src, ccol.at[p, b], chain_s.at[p, b, 1], chain_r.at[p, b], mate)
            pltpu.make_async_copy(src, ccol.at[p, b], local_sem.at[2 + p * 4 + b]).start()

    even = gap[0] == 2
    near = jnp.where(gap[0] == 3, 1, 0)
    turns = (
        ((0, 0), (0, 0)),
        ((0, 1), (1, 0)),
        ((0, 2), (0, 1)),
        ((1, 0), (1, 1)),
        ((0, 3), (0, 2)),
        ((1, 1), (1, 2)),
        ((1, 2), (0, 3)),
        ((1, 3), (1, 3)),
    )

    def relay(step):
        (side, b), (even_side, even_b) = turns[step]
        p = jnp.where(even, even_side, jnp.where(near == 1, 1 - side, side))
        b = jnp.where(even, even_b, b)
        distance = jnp.where(p == 0, gap[0], gap[1])
        onward = jnp.where(p == 0, next_y[0], next_y[1])

        @pl.when(relays)
        def _():
            held = ccol.at[p, b]
            arrived(held, chain_r.at[p, b])

            @pl.when(distance < 3)
            def _():
                send(held, held, chain_s.at[p, b, 0], chain_r.at[p, b], (onward * 2 + core, c))

            send(held, held, chain_s.at[p, b, 1], chain_r.at[p, b], mate)

    pivots = ((0, 0, 0), (1, 0, 1), (2, 1, 1))

    for slot, p, holder in pivots:

        @pl.when(r == holder)
        def _():
            src = crow.at[p, pl.ds(0, 2)]
            send(src, qbuf.at[slot], q_s.at[slot, 0], q_r.at[slot], (2 + holder, c))
            send(src, qbuf.at[slot], q_s.at[slot, 1], q_r.at[slot], (6 + holder, c))
            send(src, qbuf.at[slot], q_s.at[slot, 2], q_r.at[slot], (4 + holder, c))
            send(src, qbuf.at[slot], q_s.at[slot, 3], q_r.at[slot], mate)
            own = pltpu.make_async_copy(src, qbuf.at[slot], local_sem.at[1])
            own.start()
            own.wait()

    def adjoint_block(a, b):
        return jnp.concatenate(
            [s_ref[pl.ds(a * 2048 + 2 * b + h, 256, stride=8), :] for h in range(2)], axis=1
        )

    @pl.when(at_11)
    def _():
        rsend[...] = adjoint_block(0, 0)
        send(rsend, rblk.at[0], blk_sem.at[0], blk_sem.at[2], (0, 0))

    @pl.when(at_10)
    def _():
        rsend[...] = adjoint_block(0, 0)
        send(rsend, rblk.at[1], blk_sem.at[1], blk_sem.at[3], (0, 0))

    row_iota, col_iota = iotas((256, 256))

    def active(a, b):
        i, j = 8 * a + r, 16 * b + c
        return jnp.logical_and(j >= 2, j <= i)

    macc[...] = jnp.zeros_like(macc)

    def mirrored(a):
        for p in range(2):
            for half in range(2):
                high, low = split(crow[p, 2 * a + half])
                lanes = pl.ds(128 * half, 128)
                ct[0, pl.ds(256 * p, 256), lanes] = high.T
                ct[1, pl.ds(256 * p, 256), lanes] = low.T

        def per_block(b, carry):
            @pl.when(active(a, b))
            def _():
                shift = 256 * (8 * a + r - 16 * b - c)
                block = jnp.where(row_iota + shift >= col_iota, adjoint_block(a, b), 0.0)
                high, low = split(block)
                sw[0, a, b] = high
                sw[1, a, b] = low
                total = dot3((ct[0], ct[1]), (high, low))
                macc[b, 0] += total[:, :128]
                macc[b, 1] += total[:, 128:]

            return carry

        lax.fori_loop(0, 4, per_block, 0)

    for step in range(8):
        mirrored(step)
        relay(step)

    for b in range(4):
        post(
            macc.at[b, 1 - core], mate_in.at[b], mate_sem.at[0, b], mate_sem.at[1, b], mate
        )

    @pl.when(is_home)
    def _():
        for p, b in chunks:
            pltpu.make_async_copy(home_pieces(p, b), ccol.at[p, b], local_sem.at[2 + p * 4 + b]).wait()

    @pl.when(jnp.logical_not(in_line))
    def _():
        for p, b in chunks:
            arrived(ccol.at[p, b], chain_r.at[p, b])

    def ready_columns(b, carry):
        for p in range(2):
            for half in range(2):
                high, low = split(ccol[p, b, half])
                rows, lanes = pl.ds(128 * half, 128), pl.ds(256 * p, 256)
                cc[0, b, rows, lanes] = high
                cc[1, b, rows, lanes] = low
        return carry

    lax.fori_loop(0, 4, ready_columns, 0)

    oacc[...] = jnp.zeros_like(oacc)

    def direct(a, carry):
        for p in range(2):

            @pl.when(c == p)
            def _():
                block = adjoint_block(a, 0)
                oacc[p, 2 * a] = -block[:128]
                oacc[p, 2 * a + 1] = -block[128:]

        def per_block(b, inner):
            @pl.when(active(a, b))
            def _():
                total = dot3((sw[0, a, b], sw[1, a, b]), (cc[0, b], cc[1, b]))
                for p in range(2):
                    for half in range(2):
                        oacc[p, 2 * a + half] += total[128 * half : 128 * half + 128, 256 * p : 256 * p + 256]

            return inner

        lax.fori_loop(0, 4, per_block, 0)
        return carry

    lax.fori_loop(0, 8, direct, 0)

    def ring_open(slot, held, pos, device, rows, opp, nbr):
        def part(ref, half):
            return ref.at[pl.ds(rows * half, rows)]

        def go(src, dst, n, where):
            post(src, dst, ring.at[0, slot, n], ring.at[1, slot, n], device(where))

        far = held(across_from(pos))
        go(part(far, 0), opp.at[0], 0, down(pos))
        go(part(far, 1), opp.at[1], 1, up(pos))
        go(part(held(down(pos)), 1), part(nbr.at[0], 1), 2, down(pos))
        go(part(held(up(pos)), 0), part(nbr.at[1], 0), 3, up(pos))

    def ring_pass(slot, held, pos, device, rows, opp, nbr):
        def part(ref, half):
            return ref.at[pl.ds(rows * half, rows)]

        def go(src, dst, n, where):
            post(src, dst, ring.at[0, slot, n], ring.at[1, slot, n], device(where))

        arrived(opp.at[0], ring.at[1, slot, 0])
        mine = part(held(down(pos)), 0)
        mine[...] = mine[...] + opp[0]
        go(mine, part(nbr.at[0], 0), 4, down(pos))
        arrived(opp.at[1], ring.at[1, slot, 1])
        mine = part(held(up(pos)), 1)
        mine[...] = mine[...] + opp[1]
        go(mine, part(nbr.at[1], 1), 5, up(pos))

    def ring_close(slot, held, pos, device, rows, opp, nbr):
        def part(ref, half):
            return ref.at[pl.ds(rows * half, rows)]

        arrived(part(nbr.at[0], 1), ring.at[1, slot, 2])
        arrived(part(nbr.at[0], 0), ring.at[1, slot, 4])
        arrived(part(nbr.at[1], 0), ring.at[1, slot, 3])
        arrived(part(nbr.at[1], 1), ring.at[1, slot, 5])
        mine = held(pos)
        mine[...] = mine[...] + (nbr[0] + nbr[1])

    def first_ring(p, j):
        f, s = place[p]
        return (
            4 * p + j,
            lambda t: oacc.at[p, piece(p, j, t)],
            s,
            lambda t: member(p, f, t),
            64,
            opp1.at[p, j],
            nbr1.at[p, j],
        )

    def second_ring(p):
        f, s = place[p]
        return (
            8 + p,
            lambda t: oacc.at[p, piece(p, t, s)],
            f,
            lambda t: member(p, t, s),
            64,
            opp2.at[p],
            nbr2.at[p],
        )

    column_ring = (
        10,
        lambda t: macc.at[t, core],
        y,
        lambda t: (t * 2 + core, c),
        256,
        yopp,
        ynbr,
    )
    rings = [first_ring(p, j) for j in range(4) for p in range(2)]
    for spec in rings:
        ring_open(*spec)

    for b in range(4):
        arrived(mate_in.at[b], mate_sem.at[1, b])
    for b in range(4):
        mine = macc.at[b, core]
        mine[...] = mine[...] + mate_in[b]
    ring_open(*column_ring)

    for spec in rings:
        ring_pass(*spec)
    ring_pass(*column_ring)

    for slot, p, holder in pivots:

        @pl.when(r != holder)
        def _():
            arrived(qbuf.at[slot], q_r.at[slot])

            @pl.when(core == holder)
            def _():
                send(qbuf.at[slot], qbuf.at[slot], q_s.at[slot, 3], q_r.at[slot], mate)

    def pivot(slot):
        return jnp.concatenate([qbuf[slot, 0], qbuf[slot, 1]], axis=0)

    inverse_0, inverse_1 = inverses([pivot(0), pivot(2)])
    qinv[0] = inverse_0
    qinv[1] = inverse_1

    for spec in rings:
        ring_close(*spec)
    for p in range(2):
        ring_open(*second_ring(p))
    ring_close(*column_ring)

    @pl.when(away)
    def _():
        send(macc.at[y, core], moved, moved_sem.at[0], moved_sem.at[1], target)

    @pl.when(jnp.logical_not(away))
    def _():
        moved[...] = macc[y, core]

    for p in range(2):
        ring_pass(*second_ring(p))
    for p in range(2):
        ring_close(*second_ring(p))

    @pl.when(from_away)
    def _():
        arrived(moved, moved_sem.at[1])

    keep = jnp.where(jnp.logical_and(c < 2, r < 2), 0.0, -1.0)
    extra = moved[...].T
    sums_1 = (oacc[1, c] + extra[:, 256:]) * keep
    sums_0 = (oacc[0, c] + extra[:, :256]) * keep
    solved_1 = exact(sums_1, qinv[1])
    apiece[1] = solved_1

    def hand_in(p):
        @pl.when(c != p)
        def _():
            send(apiece.at[p], agath.at[c], ga_s.at[p], ga_r.at[c], (r, p))

    solved_0 = exact(sums_0 - exact(solved_1, pivot(1)), qinv[0])
    apiece[0] = solved_0

    sides_1, sides_0 = [tuple(v.T for v in split(m)) for m in (solved_1, solved_0)]
    right_1, right_0 = split(crow[1, c]), split(crow[0, c])
    for n, term in enumerate((dot3(sides_1, right_1), dot3(sides_1, right_0), dot3(sides_0, right_0))):
        for t in range(8):
            tpart[t, n] = term[32 * t : 32 * t + 32]
    for step in range(1, 8):
        to = lax.rem(r + step, 8)
        post(tpart.at[to], tin1.at[step], t1.at[0, step], t1.at[1, step], (to, c))
    hand_in(1)
    hand_in(0)
    result = tpart[r]
    for step in range(1, 8):
        arrived(tin1.at[step], t1.at[1, step])
        result = result + tin1[step]
    for t in range(4):
        tsum[t] = result[:, 8 * t : 8 * t + 8]
    for step in range(1, 4):
        to = lax.rem(x + step, 4)
        post(tsum.at[to], tin2.at[step], t2.at[0, step], t2.at[1, step], (r, 4 * z + to))
    result = tsum[x]
    for step in range(1, 4):
        arrived(tin2.at[step], t2.at[1, step])
        result = result + tin2[step]
    tslice[...] = result

    @pl.when(z != 0)
    def _():
        send(tslice, tin3.at[z], t3.at[0], t3.at[z], (r, x))

    @pl.when(z == 0)
    def _():
        total = result
        for n in range(1, 4):
            arrived(tin3.at[n], t3.at[n])
            total = total + tin3[n]
        tslice[...] = total

        @pl.when(jnp.logical_not(is_root))
        def _():
            send(tslice, tall.at[r, x], t3.at[0], troot.at[r, x], (0, 0))

    def flat(parts):
        return jnp.concatenate(parts, axis=0)

    @pl.when(is_root)
    def _():
        tall[0, 0] = tslice[...]
        for t in range(8):
            for n in range(4):
                if t + n > 0:
                    arrived(tall.at[t, n], troot.at[t, n])
        arrived(rblk.at[0], blk_sem.at[2])
        arrived(rblk.at[1], blk_sem.at[3])

        def total(n):
            return flat([tall[t, m, n] for t in range(8) for m in range(4)])

        diag_1 = diag_step(pivot(2), qinv[1], lower(rblk[0] - total(0)))
        rblk[0] = diag_1
        send(rblk.at[0], a01, blk_sem.at[6], blk_sem.at[5], (1, 1))
        link = pivot(1)
        rows_1 = exact(rblk[1] - total(1) - exact(diag_1 + diag_1.T, link), qinv[0])
        rsend[...] = rows_1
        send(rsend, a01, blk_sem.at[4], blk_sem.at[5], (1, 0))
        sums = total(2) + exact(rows_1.T, link)
        done[...] = diag_step(pivot(0), qinv[0], lower(adjoint_block(0, 0) - sums))
        left(rsend, blk_sem.at[4])
        left(rblk.at[0], blk_sem.at[6])

    for p in range(2):

        @pl.when(c == p)
        def _():
            agath[p] = apiece[p]
            for k in range(16):
                if k != p:
                    arrived(agath.at[k], ga_r.at[k])

    @pl.when(jnp.logical_or(at_10, at_11))
    def _():
        arrived(a01, blk_sem.at[5])
        done[...] = a01[...]

    @pl.when(c < 2)
    def _():
        def write(k, carry):
            value = agath[k]
            for h in range(2):
                out[pl.ds(256 * k + h, 128, stride=2), :] = value[:, 128 * h : 128 * h + 128]
            return carry

        lax.fori_loop(0, 16, write, 0)

        @pl.when(jnp.logical_and(r < 2, jnp.logical_or(r == 1, c == 0)))
        def _():
            value = done[...]
            for h in range(2):
                out[pl.ds(h, 256, stride=2), :] = value[:, 128 * h : 128 * h + 128]

    @pl.when(c >= 2)
    def _():
        out[...] = jnp.zeros_like(out)

    for copy in pending:
        copy.wait_send()
    for p in range(2):

        @pl.when(c == p)
        def _():
            for k in range(16):
                if k != p:
                    left(panel.at[k], scat_s.at[k])

        @pl.when(c != p)
        def _():
            left(apiece.at[p], ga_s.at[p])

    for p, b in chunks:

        @pl.when(in_line)
        def _():
            left(ccol.at[p, b], chain_s.at[p, b, 1])

            @pl.when(gap[p] < 3)
            def _():
                left(ccol.at[p, b], chain_s.at[p, b, 0])

    for slot, p, holder in pivots:

        @pl.when(core == holder)
        def _():
            left(qbuf.at[slot], q_s.at[slot, 3])

        @pl.when(r == holder)
        def _():
            for n in range(3):
                left(qbuf.at[slot], q_s.at[slot, n])

    @pl.when(at_11)
    def _():
        left(rsend, blk_sem.at[0])

    @pl.when(at_10)
    def _():
        left(rsend, blk_sem.at[1])

    @pl.when(away)
    def _():
        left(moved, moved_sem.at[0])

    @pl.when(jnp.logical_not(is_root))
    def _():
        left(tslice, t3.at[0])


def sweep(factor, adj):
    vmem = pltpu.VMEM
    dma = pltpu.SemaphoreType.DMA
    return pl.pallas_call(
        sweep_kernel,
        out_shape=jax.ShapeDtypeStruct((4096, 128), F32),
        in_specs=[pl.BlockSpec(memory_space=pl.ANY)] * 2,
        out_specs=pl.BlockSpec(memory_space=pltpu.VMEM),
        scratch_shapes=[
            vmem((16384, 128), F32),
            vmem((16, 128, 256), F32),
            vmem((2, 16, 128, 256), F32),
            vmem((2, 4, 2, 128, 256), F32),
            vmem((2, 512, 256), BF16),
            vmem((2, 8, 4, 256, 256), BF16),
            vmem((2, 4, 256, 512), BF16),
            vmem((2, 16, 128, 256), F32),
            vmem((4, 2, 512, 128), F32),
            vmem((4, 512, 128), F32),
            vmem((2, 256, 128), F32),
            vmem((2, 512, 128), F32),
            vmem((512, 128), F32),
            vmem((2, 4, 2, 64, 256), F32),
            vmem((2, 4, 2, 128, 256), F32),
            vmem((2, 2, 64, 256), F32),
            vmem((2, 2, 128, 256), F32),
            vmem((16, 128, 256), F32),
            vmem((2, 128, 256), F32),
            vmem((3, 2, 128, 256), F32),
            vmem((2, 256, 256), F32),
            vmem((8, 3, 32, 256), F32),
            vmem((8, 3, 32, 256), F32),
            vmem((4, 3, 8, 256), F32),
            vmem((4, 3, 8, 256), F32),
            vmem((3, 8, 256), F32),
            vmem((4, 3, 8, 256), F32),
            vmem((8, 4, 3, 8, 256), F32),
            vmem((2, 256, 256), F32),
            vmem((256, 256), F32),
            vmem((256, 256), F32),
            vmem((256, 256), F32),
            dma((10,)),
            dma((16,)),
            dma((2,)),
            dma((2, 2, 4)),
            dma((2, 2, 4, 4)),
            dma((2, 4, 2)),
            dma((2, 4)),
            dma((3, 4)),
            dma((3,)),
            dma((2, 11, 6)),
            dma((2, 4)),
            dma((2,)),
            dma((2,)),
            dma((16,)),
            dma((2, 8)),
            dma((2, 4)),
            dma((4,)),
            dma((8, 4)),
            dma((7,)),
        ],
        compiler_params=pltpu.CompilerParams(
            collective_id=0, has_side_effects=True, vmem_limit_bytes=60 * 2**20
        ),
        name="sweep",
    )(factor, adj)


def merge_kernel(adj, panel, out):
    r, c = lax.axis_index("row"), lax.axis_index("col")
    a = pl.program_id(0)
    shape = (256, 8, 128)
    slot = lax.broadcasted_iota(jnp.int32, (1, 8, 128), 1)
    lane = lax.broadcasted_iota(jnp.int32, (1, 8, 128), 2)
    col = (16 * (slot // 2) + c) * 256 + lax.rem(slot, 2) * 128 + lane
    row = (8 * a + r) * 256 + lax.broadcasted_iota(jnp.int32, shape, 0)
    value = jnp.where(row >= col, adj[...].reshape(shape), 0.0)
    out[...] = value.reshape(2048, 128)

    @pl.when(c < 2)
    def _():
        for h in range(2):
            out[pl.ds(h, 256, stride=8), :] = panel[pl.ds(h, 256, stride=2), :]


def merge(adj, panel):
    return pl.pallas_call(
        merge_kernel,
        grid=(8,),
        out_shape=jax.ShapeDtypeStruct((16384, 128), F32),
        in_specs=[
            pl.BlockSpec((2048, 128), lambda a: (a, 0)),
            pl.BlockSpec((512, 128), lambda a: (a, 0)),
        ],
        out_specs=pl.BlockSpec((2048, 128), lambda a: (a, 0)),
        compiler_params=pltpu.CompilerParams(vmem_limit_bytes=60 * 2**20),
        name="merge",
    )(adj, panel)


def shards(factor, adjoint):
    adj = adjoint.reshape(16384, 128)
    solved = sweep(factor.reshape(16384, 128), adj)
    return merge(adj, solved).reshape(adjoint.shape)


def solution(mesh):
    spec = P(None, "row", None, None, "col", None)
    return jax.shard_map(
        shards,
        mesh=mesh,
        in_specs=(spec, spec),
        out_specs=spec,
        check_vma=False,
    )
```

```python
import jax
import jax.numpy as jnp
from jax import lax
from jax.experimental import pallas as pl
from jax.experimental.pallas import tpu as pltpu
from jax.sharding import PartitionSpec as P

F32, BF16 = jnp.float32, jnp.bfloat16
MESH = pl.DeviceIdType.MESH
precise = lax.Precision.HIGHEST
WAVES = 1


def up(v):
    return lax.rem(v + 1, 4)


def down(v):
    return lax.rem(v + 3, 4)


def across_from(v):
    return lax.rem(v + 2, 4)


def split(value):
    high = value.astype(BF16)
    return high, (value - high.astype(F32)).astype(BF16)


def dot(left, right):
    return jnp.dot(left, right, preferred_element_type=F32)


def dot3(left, right):
    (left_high, left_low), (right_high, right_low) = left, right
    return dot(left_high, right_high) + (dot(left_high, right_low) + dot(left_low, right_high))


def exact(left, right):
    return jnp.dot(left, right, precision=precise, preferred_element_type=F32)


def iotas(shape):
    return (
        lax.broadcasted_iota(jnp.int32, shape, 0),
        lax.broadcasted_iota(jnp.int32, shape, 1),
    )


def lower(matrix):
    row, col = iotas(matrix.shape)
    return jnp.where(row >= col, matrix, 0.0)


def halve_diag(matrix):
    row, col = iotas(matrix.shape)
    return jnp.where(row > col, matrix, jnp.where(row == col, 0.5 * matrix, 0.0))


def inverses(blocks):
    row, col = iotas(blocks[0].shape)
    found = [jnp.where(row == col, 1.0 / jnp.where(row == col, q, 1.0), 0.0) for q in blocks]
    size = 1
    while size < blocks[0].shape[0]:
        here = jnp.logical_and(row // (2 * size) == col // (2 * size), row // size > col // size)
        left = [exact(x, jnp.where(here, q, 0.0)) for x, q in zip(found, blocks)]
        found = [x - exact(y, x) for x, y in zip(found, left)]
        size *= 2
    return found


def times(left, right):
    return dot3(left if isinstance(left, tuple) else split(left), right if isinstance(right, tuple) else split(right))


def turned(parts):
    return tuple(part.T for part in parts)


def diag_step(pivot, inverse, target):
    inner = halve_diag(times(pivot, target))
    return halve_diag(times(times(turned(inverse), inner), inverse))


def sweep_kernel(
    factor,
    adj,
    out,
    s_ref,
    panel,
    crow,
    ccol,
    stage,
    ct,
    sw,
    cc,
    oacc,
    macc,
    mate_in,
    yopp,
    ynbr,
    moved,
    opp1,
    nbr1,
    near,
    agath,
    apiece,
    qbuf,
    qinv,
    tpart,
    tin1,
    tsum,
    tin2,
    tslice,
    tin3,
    tall,
    rblk,
    rsend,
    done,
    a01,
    local_sem,
    scat_s,
    scat_r,
    ag1,
    ag2,
    stage_s,
    stage_r,
    col_sem,
    q_s,
    q_r,
    ring,
    ring2,
    mate_sem,
    moved_sem,
    ga_s,
    ga_r,
    t1,
    t2,
    t3,
    troot,
    blk_sem,
):
    r, c = lax.axis_index("row"), lax.axis_index("col")
    y, core = lax.div(r, 2), lax.rem(r, 2)
    z, x = lax.div(c, 4), lax.rem(c, 4)
    place = ((x, z), (z, x))
    home = lax.rem(c, 8)
    home_y, home_core = lax.div(home, 2), lax.rem(home, 2)
    group = lax.div(c, 8)
    mate = (y * 2 + 1 - core, c)
    target = (home, 4 * y + 2 * group + core)
    giver = (2 * z + lax.rem(x, 2), r + 8 * lax.div(x, 2))
    pending = []

    def piece(p, first, second):
        return second * 4 + first if p == 0 else first * 4 + second

    def member(p, first, second):
        return (r, piece(p, first, second))

    def send(src, dst, ss, rs, device):
        copy = pltpu.make_async_remote_copy(
            src_ref=src, dst_ref=dst, send_sem=ss, recv_sem=rs, device_id=device, device_id_type=MESH
        )
        copy.start()
        return copy

    def post(*args):
        pending.append(send(*args))

    def arrived(dst, rs):
        pltpu.make_async_remote_copy(
            src_ref=dst, dst_ref=dst, send_sem=rs, recv_sem=rs, device_id=mate, device_id_type=MESH
        ).wait_recv()

    def left(src, ss):
        pltpu.make_async_remote_copy(
            src_ref=src, dst_ref=src, send_sem=ss, recv_sem=ss, device_id=mate, device_id_type=MESH
        ).wait_send()

    holds_panel = c < 2
    load = pltpu.make_async_copy(adj, s_ref, local_sem.at[0])

    @pl.when(holds_panel)
    def _():
        pltpu.make_async_copy(factor, s_ref, local_sem.at[1]).start()

    barrier = pltpu.get_barrier_semaphore()

    def greet(device):
        pl.semaphore_signal(barrier, inc=1, device_id=device, device_id_type=MESH)

    for step in range(1, 16):
        greet((r, lax.rem(c + step, 16)))
    for step in range(1, 8):
        greet((lax.rem(r + step, 8), c))
    away = jnp.logical_or(target[0] != r, target[1] != c)
    from_away = jnp.logical_or(giver[0] != r, giver[1] != c)
    is_root = jnp.logical_and(r == 0, c == 0)
    owes_root = jnp.logical_and(r > 0, jnp.logical_and(c > 0, c < 4))
    at_11 = jnp.logical_and(r == 1, c == 1)
    at_10 = jnp.logical_and(r == 1, c == 0)

    @pl.when(from_away)
    def _():
        greet(giver)

    @pl.when(away)
    def _():
        greet(target)

    @pl.when(is_root)
    def _():
        for step in range(1, 8):
            for other in range(1, 4):
                greet((step, other))

    @pl.when(at_11)
    def _():
        greet((0, 0))

    @pl.when(holds_panel)
    def _():
        pltpu.make_async_copy(factor, s_ref, local_sem.at[1]).wait()

        def take(k, carry):
            for h in range(2):
                panel[k, :, pl.ds(128 * h, 128)] = s_ref[pl.ds(k * 1024 + h, 128, stride=8), :]
            return carry

        lax.fori_loop(0, 16, take, 0)

    load.start()
    pl.semaphore_wait(
        barrier,
        22
        + jnp.where(away, 1, 0)
        + jnp.where(from_away, 1, 0)
        + jnp.where(owes_root, 1, 0)
        + jnp.where(is_root, 1, 0),
    )

    orders = (
        (9, 10, 15, 8, 11, 7, 6, 14, 2, 5, 13, 3, 4, 12, 1),
        (8, 11, 14, 9, 10, 6, 7, 15, 3, 4, 12, 2, 5, 13, 0),
    )
    groups = (
        {4: (9, 8, 6, 5), 12: (10, 11, 14, 13), 3: (15, 7, 2)},
        {5: (8, 9, 7, 4), 13: (11, 10, 15, 12), 2: (14, 6, 3)},
    )
    relays = [
        {k: (via, slot) for via, members in g.items() for slot, k in enumerate(members)} for g in groups
    ]
    rows = 128 // WAVES

    def wave(ref, w):
        return ref.at[pl.ds(rows * w, rows)]

    for w in range(WAVES):
        for p in range(2):

            @pl.when(c == p)
            def _():
                for k in orders[p]:
                    src = wave(panel.at[k], w)
                    if k in relays[p]:
                        via, slot = relays[p][k]
                        send(src, stage.at[slot, w], scat_s.at[k, w], stage_r.at[slot, w], (r, via))
                    else:
                        send(src, wave(crow.at[p, k], w), scat_s.at[k, w], scat_r.at[p, w], (r, k))

    for p in range(2):

        @pl.when(c == p)
        def _():
            own = pltpu.make_async_copy(panel.at[p], crow.at[p, p], local_sem.at[1])
            own.start()
            own.wait()

    def pass_on(w):
        for p in range(2):
            for via, members in groups[p].items():

                @pl.when(c == via)
                def _():
                    for slot, k in enumerate(members):
                        held = stage.at[slot, w]
                        arrived(held, stage_r.at[slot, w])
                        send(held, wave(crow.at[p, k], w), stage_s.at[slot, w], scat_r.at[p, w], (r, k))

    def quarter(p, k, w, half):
        return crow.at[p, k, pl.ds(rows * w + rows // 2 * half, rows // 2)]

    def gather_second(p, w, q, first):
        f, s = place[p]
        held = wave(crow.at[p, piece(p, first, s)], w)
        post(held, held, ag2.at[0, w, p, q, 0], ag2.at[1, w, p, q, 0], member(p, f, up(s)))
        post(held, held, ag2.at[0, w, p, q, 1], ag2.at[1, w, p, q, 1], member(p, f, down(s)))

    def gather_open(w):
        for p in range(2):
            f, s = place[p]
            held = wave(crow.at[p, piece(p, f, s)], w)

            @pl.when(c != p)
            def _():
                arrived(wave(crow.at[p, c], w), scat_r.at[p, w])

            post(held, held, ag1.at[0, w, p, 0], ag1.at[1, w, p, 0], member(p, up(f), s))
            post(held, held, ag1.at[0, w, p, 1], ag1.at[1, w, p, 1], member(p, down(f), s))
            gather_second(p, w, 0, f)

    def gather_first(w):
        for p in range(2):
            f, s = place[p]
            k = piece(p, down(f), s)
            arrived(wave(crow.at[p, k], w), ag1.at[1, w, p, 0])
            part = quarter(p, k, w, 0)
            post(part, part, ag1.at[0, w, p, 2], ag1.at[1, w, p, 2], member(p, up(f), s))
            gather_second(p, w, 1, down(f))
            k = piece(p, up(f), s)
            arrived(wave(crow.at[p, k], w), ag1.at[1, w, p, 1])
            part = quarter(p, k, w, 1)
            post(part, part, ag1.at[0, w, p, 3], ag1.at[1, w, p, 3], member(p, down(f), s))
            gather_second(p, w, 2, up(f))
        for p in range(2):
            f, s = place[p]
            k = piece(p, across_from(f), s)
            arrived(quarter(p, k, w, 0), ag1.at[1, w, p, 2])
            arrived(quarter(p, k, w, 1), ag1.at[1, w, p, 3])
            gather_second(p, w, 3, across_from(f))

    def firsts(f):
        return f, down(f), up(f), across_from(f)

    def gather_relay(w, q):
        for p in range(2):
            f, s = place[p]
            first = firsts(f)[q]
            k = piece(p, first, down(s))
            arrived(wave(crow.at[p, k], w), ag2.at[1, w, p, q, 0])
            part = quarter(p, k, w, 0)
            post(part, part, ag2.at[0, w, p, q, 2], ag2.at[1, w, p, q, 2], member(p, f, up(s)))
            k = piece(p, first, up(s))
            arrived(wave(crow.at[p, k], w), ag2.at[1, w, p, q, 1])
            part = quarter(p, k, w, 1)
            post(part, part, ag2.at[0, w, p, q, 3], ag2.at[1, w, p, q, 3], member(p, f, down(s)))

    def gather_close(w):
        for q in range(4):
            for p in range(2):
                f, s = place[p]
                k = piece(p, firsts(f)[q], across_from(s))
                arrived(quarter(p, k, w, 0), ag2.at[1, w, p, q, 2])
                arrived(quarter(p, k, w, 1), ag2.at[1, w, p, q, 3])

    here = ccol.at[y, core]

    def to_mate(n, slot):
        post(slot, slot, col_sem.at[0, n], col_sem.at[1, n], mate)

    def column_send():
        own = crow.at[:, c]

        @pl.when(from_away)
        def _():
            send(own, ccol.at[z, lax.rem(x, 2)], col_sem.at[0, 0], col_sem.at[1, 0], giver)

        @pl.when(jnp.logical_not(from_away))
        def _():
            copy = pltpu.make_async_copy(own, here, local_sem.at[1])
            copy.start()
            copy.wait()

    def column_open():
        @pl.when(away)
        def _():
            arrived(here, col_sem.at[1, 0])

        post(here, here, col_sem.at[0, 1], col_sem.at[1, 1], (up(y) * 2 + core, c))
        post(here, here, col_sem.at[0, 2], col_sem.at[1, 2], (down(y) * 2 + core, c))
        to_mate(5, here)

    def column_relay():
        slot = ccol.at[down(y), core]
        arrived(slot, col_sem.at[1, 1])
        post(slot.at[0], slot.at[0], col_sem.at[0, 3], col_sem.at[1, 3], (up(y) * 2 + core, c))
        to_mate(6, slot)
        slot = ccol.at[up(y), core]
        arrived(slot, col_sem.at[1, 2])
        post(slot.at[1], slot.at[1], col_sem.at[0, 4], col_sem.at[1, 4], (down(y) * 2 + core, c))
        to_mate(7, slot)

    def column_close():
        slot = ccol.at[across_from(y), core]
        arrived(slot.at[0], col_sem.at[1, 3])
        arrived(slot.at[1], col_sem.at[1, 4])
        to_mate(8, slot)

    def column_wait():
        for n, t in ((5, y), (6, down(y)), (7, up(y)), (8, across_from(y))):
            arrived(ccol.at[t, 1 - core], col_sem.at[1, n])

    for w in range(WAVES):
        pass_on(w)
        gather_open(w)
    column_send()
    for w in range(WAVES):
        gather_first(w)
    column_open()
    for w in range(WAVES):
        gather_relay(w, 0)
        gather_relay(w, 1)
    column_relay()
    for w in range(WAVES):
        gather_relay(w, 2)
        gather_relay(w, 3)
    column_close()
    for w in range(WAVES):
        gather_close(w)

    load.wait()

    pivots = ((0, 0, 0), (1, 0, 1), (2, 1, 1))

    for slot, p, holder in pivots:

        @pl.when(r == holder)
        def _():
            src = crow.at[p, pl.ds(0, 2)]
            send(src, qbuf.at[slot], q_s.at[slot, 0], q_r.at[slot], (2 + holder, c))
            send(src, qbuf.at[slot], q_s.at[slot, 1], q_r.at[slot], (6 + holder, c))
            send(src, qbuf.at[slot], q_s.at[slot, 2], q_r.at[slot], (4 + holder, c))
            send(src, qbuf.at[slot], q_s.at[slot, 3], q_r.at[slot], mate)
            own = pltpu.make_async_copy(src, qbuf.at[slot], local_sem.at[1])
            own.start()
            own.wait()

    def adjoint_block(a, b):
        return jnp.concatenate(
            [s_ref[pl.ds(a * 2048 + 2 * b + h, 256, stride=8), :] for h in range(2)], axis=1
        )

    @pl.when(at_11)
    def _():
        rsend[...] = adjoint_block(0, 0)
        send(rsend, rblk.at[0], blk_sem.at[0], blk_sem.at[2], (0, 0))

    @pl.when(at_10)
    def _():
        rsend[...] = adjoint_block(0, 0)
        send(rsend, rblk.at[1], blk_sem.at[1], blk_sem.at[3], (0, 0))

    row_iota, col_iota = iotas((256, 256))

    def active(a, b):
        i, j = 8 * a + r, 16 * b + c
        return jnp.logical_and(j >= 2, j <= i)

    macc[...] = jnp.zeros_like(macc)

    def mirrored(a):
        for p in range(2):
            for half in range(2):
                high, low = split(crow[p, 2 * a + half])
                lanes = pl.ds(128 * half, 128)
                ct[0, pl.ds(256 * p, 256), lanes] = high.T
                ct[1, pl.ds(256 * p, 256), lanes] = low.T

        def per_block(b, carry):
            @pl.when(active(a, b))
            def _():
                shift = 256 * (8 * a + r - 16 * b - c)
                block = jnp.where(row_iota + shift >= col_iota, adjoint_block(a, b), 0.0)
                high, low = split(block)
                sw[0, a, b] = high
                sw[1, a, b] = low
                total = dot3((ct[0], ct[1]), (high, low))
                macc[b, 0] += total[:, :128]
                macc[b, 1] += total[:, 128:]

            return carry

        lax.fori_loop(0, 4, per_block, 0)

    for step in range(8):
        mirrored(step)

    for b in range(4):
        post(
            macc.at[b, 1 - core], mate_in.at[b], mate_sem.at[0, b], mate_sem.at[1, b], mate
        )

    column_wait()

    def ready_columns(b, carry):
        for p in range(2):
            for half in range(2):
                high, low = split(ccol[b, half, p])
                rows, lanes = pl.ds(128 * half, 128), pl.ds(256 * p, 256)
                cc[0, b, rows, lanes] = high
                cc[1, b, rows, lanes] = low
        return carry

    lax.fori_loop(0, 4, ready_columns, 0)

    oacc[...] = jnp.zeros_like(oacc)

    def direct(a, carry):
        for p in range(2):

            @pl.when(c == p)
            def _():
                block = adjoint_block(a, 0)
                oacc[p, 2 * a] = -block[:128]
                oacc[p, 2 * a + 1] = -block[128:]

        def per_block(b, inner):
            @pl.when(active(a, b))
            def _():
                total = dot3((sw[0, a, b], sw[1, a, b]), (cc[0, b], cc[1, b]))
                for p in range(2):
                    for half in range(2):
                        oacc[p, 2 * a + half] += total[128 * half : 128 * half + 128, 256 * p : 256 * p + 256]

            return inner

        lax.fori_loop(0, 4, per_block, 0)
        return carry


    def ring_open(slot, held, pos, device, rows, opp, nbr, stage=None):
        def part(ref, half):
            return ref.at[pl.ds(rows * half, rows)]

        def go(src, dst, n, where):
            post(src, dst, ring.at[0, slot, n], ring.at[1, slot, n], device(where))

        if stage in (None, 0):
            far = held(across_from(pos))
            go(part(far, 0), opp.at[0], 0, down(pos))
            go(part(far, 1), opp.at[1], 1, up(pos))
        if stage in (None, 1):
            go(part(held(up(pos)), 0), part(nbr.at[1], 0), 3, up(pos))
        if stage in (None, 2):
            go(part(held(down(pos)), 1), part(nbr.at[0], 1), 2, down(pos))

    def ring_pass(slot, held, pos, device, rows, opp, nbr):
        def part(ref, half):
            return ref.at[pl.ds(rows * half, rows)]

        def go(src, dst, n, where):
            post(src, dst, ring.at[0, slot, n], ring.at[1, slot, n], device(where))

        arrived(opp.at[0], ring.at[1, slot, 0])
        mine = part(held(down(pos)), 0)
        mine[...] = mine[...] + opp[0]
        go(mine, part(nbr.at[0], 0), 4, down(pos))
        arrived(opp.at[1], ring.at[1, slot, 1])
        mine = part(held(up(pos)), 1)
        mine[...] = mine[...] + opp[1]
        go(mine, part(nbr.at[1], 1), 5, up(pos))

    def ring_close(slot, held, pos, device, rows, opp, nbr):
        def part(ref, half):
            return ref.at[pl.ds(rows * half, rows)]

        arrived(part(nbr.at[0], 1), ring.at[1, slot, 2])
        arrived(part(nbr.at[0], 0), ring.at[1, slot, 4])
        arrived(part(nbr.at[1], 0), ring.at[1, slot, 3])
        arrived(part(nbr.at[1], 1), ring.at[1, slot, 5])
        mine = held(pos)
        mine[...] = mine[...] + (nbr[0] + nbr[1])

    def first_ring(p, j):
        f, s = place[p]
        return (
            4 * p + j,
            lambda t: oacc.at[p, piece(p, j, t)],
            s,
            lambda t: member(p, f, t),
            64,
            opp1.at[p, j],
            nbr1.at[p, j],
        )

    def second_open(p):
        f, s = place[p]
        for n, hop in enumerate((across_from, up, down)):
            to = hop(f)
            post(
                oacc.at[p, piece(p, to, s)],
                near.at[p, n],
                ring2.at[0, p, n],
                ring2.at[1, p, n],
                member(p, to, s),
            )

    def second_close(p):
        for n in range(3):
            arrived(near.at[p, n], ring2.at[1, p, n])
        return oacc[p, c] + (near[p, 0] + (near[p, 1] + near[p, 2]))

    column_ring = (
        10,
        lambda t: macc.at[t, core],
        y,
        lambda t: (t * 2 + core, c),
        256,
        yopp,
        ynbr,
    )
    groups_of_rows = (across_from(z), up(z), down(z), z)
    for n, owner in enumerate(groups_of_rows):
        lax.fori_loop(2 * owner, 2 * owner + 2, direct, 0)
        ring_open(*first_ring(1, owner))
        if n < 3:
            for j in range(4):
                ring_open(*first_ring(0, j), stage=n)
    rings = [ring for n in range(4) for ring in (first_ring(0, n), first_ring(1, groups_of_rows[n]))]

    for b in range(4):
        arrived(mate_in.at[b], mate_sem.at[1, b])
    for b in range(4):
        mine = macc.at[b, core]
        mine[...] = mine[...] + mate_in[b]
    ring_open(*column_ring)

    for spec in rings:
        ring_pass(*spec)
    ring_pass(*column_ring)

    for slot, p, holder in pivots:

        @pl.when(r != holder)
        def _():
            arrived(qbuf.at[slot], q_r.at[slot])

            @pl.when(core == holder)
            def _():
                send(qbuf.at[slot], qbuf.at[slot], q_s.at[slot, 3], q_r.at[slot], mate)

    def pivot(slot):
        return jnp.concatenate([qbuf[slot, 0], qbuf[slot, 1]], axis=0)

    inverse_0, inverse_1 = inverses([pivot(0), pivot(2)])
    qinv[0] = inverse_0
    qinv[1] = inverse_1

    for spec in rings:
        ring_close(*spec)
    for p in range(2):
        second_open(p)
    ring_close(*column_ring)

    @pl.when(away)
    def _():
        send(macc.at[y, core], moved, moved_sem.at[0], moved_sem.at[1], target)

    @pl.when(jnp.logical_not(away))
    def _():
        moved[...] = macc[y, core]

    closed_0, closed_1 = second_close(0), second_close(1)

    @pl.when(from_away)
    def _():
        arrived(moved, moved_sem.at[1])

    keep = jnp.where(jnp.logical_and(c < 2, r < 2), 0.0, -1.0)
    extra = moved[...].T
    sums_1 = (closed_1 + extra[:, 256:]) * keep
    sums_0 = (closed_0 + extra[:, :256]) * keep
    parts_1, parts_0 = split(qinv[1]), split(qinv[0])
    solved_1 = times(sums_1, parts_1)
    apiece[1] = solved_1

    def hand_in(p):
        @pl.when(c != p)
        def _():
            send(apiece.at[p], agath.at[c], ga_s.at[p], ga_r.at[c], (r, p))

    solved_0 = times(sums_0 - times(solved_1, pivot(1)), parts_0)
    apiece[0] = solved_0

    sides_1, sides_0 = [tuple(v.T for v in split(m)) for m in (solved_1, solved_0)]
    right_1, right_0 = split(crow[1, c]), split(crow[0, c])
    for n, term in enumerate((dot3(sides_1, right_1), dot3(sides_1, right_0), dot3(sides_0, right_0))):
        for t in range(8):
            tpart[t, n] = term[32 * t : 32 * t + 32]
    for step in range(1, 8):
        to = lax.rem(r + step, 8)
        post(tpart.at[to], tin1.at[step], t1.at[0, step], t1.at[1, step], (to, c))
    hand_in(1)
    hand_in(0)
    result = tpart[r]
    for step in range(1, 8):
        arrived(tin1.at[step], t1.at[1, step])
        result = result + tin1[step]
    for t in range(4):
        tsum[t] = result[:, 8 * t : 8 * t + 8]
    for step in range(1, 4):
        to = lax.rem(x + step, 4)
        post(tsum.at[to], tin2.at[step], t2.at[0, step], t2.at[1, step], (r, 4 * z + to))
    result = tsum[x]
    for step in range(1, 4):
        arrived(tin2.at[step], t2.at[1, step])
        result = result + tin2[step]
    tslice[...] = result

    @pl.when(z != 0)
    def _():
        send(tslice, tin3.at[z], t3.at[0], t3.at[z], (r, x))

    @pl.when(z == 0)
    def _():
        total = result
        for n in range(1, 4):
            arrived(tin3.at[n], t3.at[n])
            total = total + tin3[n]
        tslice[...] = total

        @pl.when(jnp.logical_not(is_root))
        def _():
            send(tslice, tall.at[r, x], t3.at[0], troot.at[r, x], (0, 0))

    def flat(parts):
        return jnp.concatenate(parts, axis=0)

    @pl.when(is_root)
    def _():
        tall[0, 0] = tslice[...]
        link = split(pivot(1))
        pivot_1, pivot_0 = turned(split(pivot(2))), turned(split(pivot(0)))
        ahead = split(times(link, parts_0))
        for t in range(8):
            for n in range(4):
                if t + n > 0:
                    arrived(tall.at[t, n], troot.at[t, n])
        arrived(rblk.at[0], blk_sem.at[2])
        arrived(rblk.at[1], blk_sem.at[3])

        def total(n):
            return flat([tall[t, m, n] for t in range(8) for m in range(4)])

        diag_1 = diag_step(pivot_1, parts_1, lower(rblk[0] - total(0)))
        rblk[0] = diag_1
        send(rblk.at[0], a01, blk_sem.at[6], blk_sem.at[5], (1, 1))
        rows_1 = times(rblk[1] - total(1), parts_0) - times(diag_1 + diag_1.T, ahead)
        rsend[...] = rows_1
        send(rsend, a01, blk_sem.at[4], blk_sem.at[5], (1, 0))
        sums = total(2) + times(turned(split(rows_1)), link)
        done[...] = diag_step(pivot_0, parts_0, lower(adjoint_block(0, 0) - sums))
        left(rsend, blk_sem.at[4])
        left(rblk.at[0], blk_sem.at[6])

    for p in range(2):

        @pl.when(c == p)
        def _():
            agath[p] = apiece[p]
            for k in range(16):
                if k != p:
                    arrived(agath.at[k], ga_r.at[k])

    @pl.when(jnp.logical_or(at_10, at_11))
    def _():
        arrived(a01, blk_sem.at[5])
        done[...] = a01[...]

    @pl.when(c < 2)
    def _():
        def write(k, carry):
            value = agath[k]
            for h in range(2):
                out[pl.ds(256 * k + h, 128, stride=2), :] = value[:, 128 * h : 128 * h + 128]
            return carry

        lax.fori_loop(0, 16, write, 0)

        @pl.when(jnp.logical_and(r < 2, jnp.logical_or(r == 1, c == 0)))
        def _():
            value = done[...]
            for h in range(2):
                out[pl.ds(h, 256, stride=2), :] = value[:, 128 * h : 128 * h + 128]

    @pl.when(c >= 2)
    def _():
        out[...] = jnp.zeros_like(out)

    for copy in pending:
        copy.wait_send()
    for p in range(2):

        @pl.when(c == p)
        def _():
            for k in orders[p]:
                for w in range(WAVES):
                    left(wave(panel.at[k], w), scat_s.at[k, w])

        @pl.when(c != p)
        def _():
            left(apiece.at[p], ga_s.at[p])

        for via, slot in relays[p].values():

            @pl.when(c == via)
            def _():
                for w in range(WAVES):
                    left(stage.at[slot, w], stage_s.at[slot, w])

    @pl.when(from_away)
    def _():
        left(here, col_sem.at[0, 0])

    for slot, p, holder in pivots:

        @pl.when(core == holder)
        def _():
            left(qbuf.at[slot], q_s.at[slot, 3])

        @pl.when(r == holder)
        def _():
            for n in range(3):
                left(qbuf.at[slot], q_s.at[slot, n])

    @pl.when(at_11)
    def _():
        left(rsend, blk_sem.at[0])

    @pl.when(at_10)
    def _():
        left(rsend, blk_sem.at[1])

    @pl.when(away)
    def _():
        left(moved, moved_sem.at[0])

    @pl.when(jnp.logical_not(is_root))
    def _():
        left(tslice, t3.at[0])


def sweep(factor, adj):
    vmem = pltpu.VMEM
    dma = pltpu.SemaphoreType.DMA
    return pl.pallas_call(
        sweep_kernel,
        out_shape=jax.ShapeDtypeStruct((4096, 128), F32),
        in_specs=[pl.BlockSpec(memory_space=pl.ANY)] * 2,
        out_specs=pl.BlockSpec(memory_space=pltpu.VMEM),
        scratch_shapes=[
            vmem((16384, 128), F32),
            vmem((16, 128, 256), F32),
            vmem((2, 16, 128, 256), F32),
            vmem((4, 2, 2, 128, 256), F32),
            vmem((4, WAVES, 128 // WAVES, 256), F32),
            vmem((2, 512, 256), BF16),
            vmem((2, 8, 4, 256, 256), BF16),
            vmem((2, 4, 256, 512), BF16),
            vmem((2, 16, 128, 256), F32),
            vmem((4, 2, 512, 128), F32),
            vmem((4, 512, 128), F32),
            vmem((2, 256, 128), F32),
            vmem((2, 512, 128), F32),
            vmem((512, 128), F32),
            vmem((2, 4, 2, 64, 256), F32),
            vmem((2, 4, 2, 128, 256), F32),
            vmem((2, 3, 128, 256), F32),
            vmem((16, 128, 256), F32),
            vmem((2, 128, 256), F32),
            vmem((3, 2, 128, 256), F32),
            vmem((2, 256, 256), F32),
            vmem((8, 3, 32, 256), F32),
            vmem((8, 3, 32, 256), F32),
            vmem((4, 3, 8, 256), F32),
            vmem((4, 3, 8, 256), F32),
            vmem((3, 8, 256), F32),
            vmem((4, 3, 8, 256), F32),
            vmem((8, 4, 3, 8, 256), F32),
            vmem((2, 256, 256), F32),
            vmem((256, 256), F32),
            vmem((256, 256), F32),
            vmem((256, 256), F32),
            dma((10,)),
            dma((16, WAVES)),
            dma((2, WAVES)),
            dma((2, WAVES, 2, 4)),
            dma((2, WAVES, 2, 4, 4)),
            dma((4, WAVES)),
            dma((4, WAVES)),
            dma((2, 9)),
            dma((3, 4)),
            dma((3,)),
            dma((2, 11, 6)),
            dma((2, 2, 3)),
            dma((2, 4)),
            dma((2,)),
            dma((2,)),
            dma((16,)),
            dma((2, 8)),
            dma((2, 4)),
            dma((4,)),
            dma((8, 4)),
            dma((7,)),
        ],
        compiler_params=pltpu.CompilerParams(
            collective_id=0, has_side_effects=True, vmem_limit_bytes=60 * 2**20
        ),
        name="sweep",
    )(factor, adj)


def merge_kernel(adj, panel, out, held, solved, sem):
    r, c = lax.axis_index("row"), lax.axis_index("col")
    shape = (256, 8, 128)
    slot = lax.broadcasted_iota(jnp.int32, (1, 8, 128), 1)
    lane = lax.broadcasted_iota(jnp.int32, (1, 8, 128), 2)
    col = (16 * (slot // 2) + c) * 256 + lax.rem(slot, 2) * 128 + lane
    row = r * 256 + lax.broadcasted_iota(jnp.int32, shape, 0)

    def rows(ref, a):
        return ref.at[pl.ds(2048 * a, 2048)]

    def come(a):
        return pltpu.make_async_copy(rows(adj, a), held.at[a], sem.at[0, a])

    def go(a):
        return pltpu.make_async_copy(held.at[a], rows(out, a), sem.at[1, a])

    fetch = pltpu.make_async_copy(panel, solved, sem.at[2, 0])
    for a in range(8):
        come(a).start()

    @pl.when(c < 2)
    def _():
        fetch.start()
        fetch.wait()

    for a in range(8):
        come(a).wait()
        held[a] = jnp.where(row + 2048 * a >= col, held[a].reshape(shape), 0.0).reshape(2048, 128)

        @pl.when(c < 2)
        def _():
            for h in range(2):
                held[a, pl.ds(h, 256, stride=8), :] = solved[pl.ds(512 * a + h, 256, stride=2), :]

        go(a).start()
    for a in range(8):
        go(a).wait()


def merge(adj, panel):
    return pl.pallas_call(
        merge_kernel,
        out_shape=jax.ShapeDtypeStruct((16384, 128), F32),
        in_specs=[pl.BlockSpec(memory_space=pl.ANY)] * 2,
        out_specs=pl.BlockSpec(memory_space=pl.ANY),
        scratch_shapes=[
            pltpu.VMEM((8, 2048, 128), F32),
            pltpu.VMEM((4096, 128), F32),
            pltpu.SemaphoreType.DMA((3, 8)),
        ],
        compiler_params=pltpu.CompilerParams(vmem_limit_bytes=60 * 2**20),
        name="merge",
    )(adj, panel)


def shards(factor, adjoint):
    adj = adjoint.reshape(16384, 128)
    solved = sweep(factor.reshape(16384, 128), adj)
    return merge(adj, solved).reshape(adjoint.shape)


def solution(mesh):
    spec = P(None, "row", None, None, "col", None)
    return jax.shard_map(
        shards,
        mesh=mesh,
        in_specs=(spec, spec),
        out_specs=spec,
        check_vma=False,
    )
```

```python
import jax
import jax.numpy as jnp
from jax import lax
from jax.experimental import pallas as pl
from jax.experimental.pallas import tpu as pltpu
from jax.sharding import PartitionSpec as P

F32, BF16 = jnp.float32, jnp.bfloat16
MESH = pl.DeviceIdType.MESH
precise = lax.Precision.HIGHEST
WAVES = 1


def up(v):
    return lax.rem(v + 1, 4)


def down(v):
    return lax.rem(v + 3, 4)


def across_from(v):
    return lax.rem(v + 2, 4)


def split(value):
    high = value.astype(BF16)
    return high, (value - high.astype(F32)).astype(BF16)


def dot(left, right):
    return jnp.dot(left, right, preferred_element_type=F32)


def dot3(left, right):
    (left_high, left_low), (right_high, right_low) = left, right
    return dot(left_high, right_high) + (dot(left_high, right_low) + dot(left_low, right_high))


def exact(left, right):
    return jnp.dot(left, right, precision=precise, preferred_element_type=F32)


def iotas(shape):
    return (
        lax.broadcasted_iota(jnp.int32, shape, 0),
        lax.broadcasted_iota(jnp.int32, shape, 1),
    )


def lower(matrix):
    row, col = iotas(matrix.shape)
    return jnp.where(row >= col, matrix, 0.0)


def halve_diag(matrix):
    row, col = iotas(matrix.shape)
    return jnp.where(row > col, matrix, jnp.where(row == col, 0.5 * matrix, 0.0))


def inverse_open(blocks):
    row, col = iotas(blocks[0].shape)
    pair = jnp.logical_and(row // 2 == col // 2, row > col)
    found = []
    for q in blocks:
        diag = jnp.where(row == col, 1.0 / jnp.where(row == col, q, 1.0), 0.0)
        down_rows = jnp.sum(diag, axis=1, keepdims=True)
        down_cols = jnp.sum(diag, axis=0, keepdims=True)
        found.append(diag - jnp.where(pair, down_rows * q * down_cols, 0.0))
    return found


def inverse_grow(found, blocks, sizes):
    row, col = iotas(blocks[0].shape)
    for size in sizes:
        here = jnp.logical_and(row // (2 * size) == col // (2 * size), row // size > col // size)
        left = [exact(x, jnp.where(here, q, 0.0)) for x, q in zip(found, blocks)]
        found = [x - exact(y, x) for x, y in zip(found, left)]
    return found


def times(left, right):
    return dot3(left if isinstance(left, tuple) else split(left), right if isinstance(right, tuple) else split(right))


def turned(parts):
    return tuple(part.T for part in parts)


def diag_step(pivot, inverse, target):
    inner = halve_diag(times(pivot, target))
    return halve_diag(times(times(turned(inverse), inner), inverse))


def sweep_kernel(
    factor,
    adj,
    out,
    s_ref,
    panel,
    crow,
    ccol,
    stage,
    ct,
    sw,
    cc,
    oacc,
    macc,
    mate_in,
    yopp,
    ynbr,
    moved,
    opp1,
    nbr1,
    near,
    agath,
    gstage,
    apiece,
    qbuf,
    qinv,
    qwork,
    tpart,
    tin1,
    tsum,
    tin2,
    tslice,
    tin3,
    tall,
    rblk,
    rsend,
    done,
    a01,
    local_sem,
    scat_s,
    scat_r,
    ag1,
    ag2,
    stage_s,
    stage_r,
    col_sem,
    q_s,
    q_r,
    ring,
    ring2,
    mate_sem,
    moved_sem,
    ga_s,
    ga_r,
    gst_s,
    gst_r,
    t1,
    t2,
    t3,
    troot,
    blk_sem,
):
    r, c = lax.axis_index("row"), lax.axis_index("col")
    y, core = lax.div(r, 2), lax.rem(r, 2)
    z, x = lax.div(c, 4), lax.rem(c, 4)
    place = ((x, z), (z, x))
    home = lax.rem(c, 8)
    home_y, home_core = lax.div(home, 2), lax.rem(home, 2)
    group = lax.div(c, 8)
    mate = (y * 2 + 1 - core, c)
    target = (home, 4 * y + 2 * group + core)
    giver = (2 * z + lax.rem(x, 2), r + 8 * lax.div(x, 2))
    pending = []

    def piece(p, first, second):
        return second * 4 + first if p == 0 else first * 4 + second

    def member(p, first, second):
        return (r, piece(p, first, second))

    def send(src, dst, ss, rs, device):
        copy = pltpu.make_async_remote_copy(
            src_ref=src, dst_ref=dst, send_sem=ss, recv_sem=rs, device_id=device, device_id_type=MESH
        )
        copy.start()
        return copy

    def post(*args):
        pending.append(send(*args))

    def arrived(dst, rs):
        pltpu.make_async_remote_copy(
            src_ref=dst, dst_ref=dst, send_sem=rs, recv_sem=rs, device_id=mate, device_id_type=MESH
        ).wait_recv()

    def left(src, ss):
        pltpu.make_async_remote_copy(
            src_ref=src, dst_ref=src, send_sem=ss, recv_sem=ss, device_id=mate, device_id_type=MESH
        ).wait_send()

    holds_panel = c < 2
    load = pltpu.make_async_copy(adj, s_ref, local_sem.at[0])

    @pl.when(holds_panel)
    def _():
        pltpu.make_async_copy(factor, s_ref, local_sem.at[1]).start()

    barrier = pltpu.get_barrier_semaphore()

    def greet(device):
        pl.semaphore_signal(barrier, inc=1, device_id=device, device_id_type=MESH)

    for step in range(1, 16):
        greet((r, lax.rem(c + step, 16)))
    for step in range(1, 8):
        greet((lax.rem(r + step, 8), c))
    away = jnp.logical_or(target[0] != r, target[1] != c)
    from_away = jnp.logical_or(giver[0] != r, giver[1] != c)
    is_root = jnp.logical_and(r == 0, c == 0)
    owes_root = jnp.logical_and(r > 0, jnp.logical_and(c > 0, c < 4))
    at_11 = jnp.logical_and(r == 1, c == 1)
    at_10 = jnp.logical_and(r == 1, c == 0)

    @pl.when(from_away)
    def _():
        greet(giver)

    @pl.when(away)
    def _():
        greet(target)

    @pl.when(is_root)
    def _():
        for step in range(1, 8):
            for other in range(1, 4):
                greet((step, other))

    @pl.when(at_11)
    def _():
        greet((0, 0))

    @pl.when(holds_panel)
    def _():
        pltpu.make_async_copy(factor, s_ref, local_sem.at[1]).wait()

        def take(k, carry):
            for h in range(2):
                panel[k, :, pl.ds(128 * h, 128)] = s_ref[pl.ds(k * 1024 + h, 128, stride=8), :]
            return carry

        lax.fori_loop(0, 16, take, 0)

    load.start()
    pl.semaphore_wait(
        barrier,
        22
        + jnp.where(away, 1, 0)
        + jnp.where(from_away, 1, 0)
        + jnp.where(owes_root, 1, 0)
        + jnp.where(is_root, 1, 0),
    )

    orders = (
        (9, 10, 15, 8, 11, 7, 6, 14, 2, 5, 13, 3, 4, 12, 1),
        (8, 11, 14, 9, 10, 6, 7, 15, 3, 4, 12, 2, 5, 13, 0),
    )
    groups = (
        {4: (9, 8, 6, 5), 12: (10, 11, 14, 13), 3: (15, 7, 2)},
        {5: (8, 9, 7, 4), 13: (11, 10, 15, 12), 2: (14, 6, 3)},
    )
    relays = [
        {k: (via, slot) for via, members in g.items() for slot, k in enumerate(members)} for g in groups
    ]
    rows = 128 // WAVES

    def wave(ref, w):
        return ref.at[pl.ds(rows * w, rows)]

    for w in range(WAVES):
        for p in range(2):

            @pl.when(c == p)
            def _():
                for k in orders[p]:
                    src = wave(panel.at[k], w)
                    if k in relays[p]:
                        via, slot = relays[p][k]
                        send(src, stage.at[slot, w], scat_s.at[k, w], stage_r.at[slot, w], (r, via))
                    else:
                        send(src, wave(crow.at[p, k], w), scat_s.at[k, w], scat_r.at[p, w], (r, k))

    for p in range(2):

        @pl.when(c == p)
        def _():
            own = pltpu.make_async_copy(panel.at[p], crow.at[p, p], local_sem.at[1])
            own.start()
            own.wait()

    def pass_on(w):
        for p in range(2):
            for via, members in groups[p].items():

                @pl.when(c == via)
                def _():
                    for slot, k in enumerate(members):
                        held = stage.at[slot, w]
                        arrived(held, stage_r.at[slot, w])
                        send(held, wave(crow.at[p, k], w), stage_s.at[slot, w], scat_r.at[p, w], (r, k))

    def quarter(p, k, w, half):
        return crow.at[p, k, pl.ds(rows * w + rows // 2 * half, rows // 2)]

    def gather_second(p, w, q, first):
        f, s = place[p]
        held = wave(crow.at[p, piece(p, first, s)], w)
        post(held, held, ag2.at[0, w, p, q, 0], ag2.at[1, w, p, q, 0], member(p, f, up(s)))
        post(held, held, ag2.at[0, w, p, q, 1], ag2.at[1, w, p, q, 1], member(p, f, down(s)))

    def scattered(w):
        for p in range(2):

            @pl.when(c != p)
            def _():
                arrived(wave(crow.at[p, c], w), scat_r.at[p, w])

    def gather_open(w):
        for p in range(2):
            f, s = place[p]
            held = wave(crow.at[p, piece(p, f, s)], w)
            post(held, held, ag1.at[0, w, p, 0], ag1.at[1, w, p, 0], member(p, up(f), s))
            post(held, held, ag1.at[0, w, p, 1], ag1.at[1, w, p, 1], member(p, down(f), s))
            gather_second(p, w, 0, f)

    def gather_first(w):
        for p in range(2):
            f, s = place[p]
            k = piece(p, down(f), s)
            arrived(wave(crow.at[p, k], w), ag1.at[1, w, p, 0])
            part = quarter(p, k, w, 0)
            post(part, part, ag1.at[0, w, p, 2], ag1.at[1, w, p, 2], member(p, up(f), s))
            gather_second(p, w, 1, down(f))
            k = piece(p, up(f), s)
            arrived(wave(crow.at[p, k], w), ag1.at[1, w, p, 1])
            part = quarter(p, k, w, 1)
            post(part, part, ag1.at[0, w, p, 3], ag1.at[1, w, p, 3], member(p, down(f), s))
            gather_second(p, w, 2, up(f))
        for p in range(2):
            f, s = place[p]
            k = piece(p, across_from(f), s)
            arrived(quarter(p, k, w, 0), ag1.at[1, w, p, 2])
            arrived(quarter(p, k, w, 1), ag1.at[1, w, p, 3])
            gather_second(p, w, 3, across_from(f))

    def firsts(f):
        return f, down(f), up(f), across_from(f)

    def gather_relay(w, q):
        for p in range(2):
            f, s = place[p]
            first = firsts(f)[q]
            k = piece(p, first, down(s))
            arrived(wave(crow.at[p, k], w), ag2.at[1, w, p, q, 0])
            part = quarter(p, k, w, 0)
            post(part, part, ag2.at[0, w, p, q, 2], ag2.at[1, w, p, q, 2], member(p, f, up(s)))
            k = piece(p, first, up(s))
            arrived(wave(crow.at[p, k], w), ag2.at[1, w, p, q, 1])
            part = quarter(p, k, w, 1)
            post(part, part, ag2.at[0, w, p, q, 3], ag2.at[1, w, p, q, 3], member(p, f, down(s)))

    def gather_close(w):
        for q in range(4):
            for p in range(2):
                f, s = place[p]
                k = piece(p, firsts(f)[q], across_from(s))
                arrived(quarter(p, k, w, 0), ag2.at[1, w, p, q, 2])
                arrived(quarter(p, k, w, 1), ag2.at[1, w, p, q, 3])

    here = ccol.at[y, core]

    def to_mate(n, slot):
        post(slot, slot, col_sem.at[0, n], col_sem.at[1, n], mate)

    def column_send():
        own = crow.at[:, c]

        @pl.when(from_away)
        def _():
            send(own, ccol.at[z, lax.rem(x, 2)], col_sem.at[0, 0], col_sem.at[1, 0], giver)

        @pl.when(jnp.logical_not(from_away))
        def _():
            copy = pltpu.make_async_copy(own, here, local_sem.at[1])
            copy.start()
            copy.wait()

    def column_open():
        @pl.when(away)
        def _():
            arrived(here, col_sem.at[1, 0])

        post(here, here, col_sem.at[0, 1], col_sem.at[1, 1], (up(y) * 2 + core, c))
        post(here, here, col_sem.at[0, 2], col_sem.at[1, 2], (down(y) * 2 + core, c))
        to_mate(5, here)

    def column_relay():
        slot = ccol.at[down(y), core]
        arrived(slot, col_sem.at[1, 1])
        post(slot.at[0], slot.at[0], col_sem.at[0, 3], col_sem.at[1, 3], (up(y) * 2 + core, c))
        to_mate(6, slot)
        slot = ccol.at[up(y), core]
        arrived(slot, col_sem.at[1, 2])
        post(slot.at[1], slot.at[1], col_sem.at[0, 4], col_sem.at[1, 4], (down(y) * 2 + core, c))
        to_mate(7, slot)

    def column_close():
        slot = ccol.at[across_from(y), core]
        arrived(slot.at[0], col_sem.at[1, 3])
        arrived(slot.at[1], col_sem.at[1, 4])
        to_mate(8, slot)

    def column_wait():
        for n, t in ((5, y), (6, down(y)), (7, up(y)), (8, across_from(y))):
            arrived(ccol.at[t, 1 - core], col_sem.at[1, n])

    def adjoint_block(a, b):
        return jnp.concatenate(
            [s_ref[pl.ds(a * 2048 + 2 * b + h, 256, stride=8), :] for h in range(2)], axis=1
        )

    row_iota, col_iota = iotas((256, 256))

    def active(a, b):
        i, j = 8 * a + r, 16 * b + c
        return jnp.logical_and(j >= 2, j <= i)

    macc[...] = jnp.zeros_like(macc)

    def mirrored(a):
        for p in range(2):
            for half in range(2):
                high, low = split(crow[p, 2 * a + half])
                lanes = pl.ds(128 * half, 128)
                ct[0, pl.ds(256 * p, 256), lanes] = high.T
                ct[1, pl.ds(256 * p, 256), lanes] = low.T

        def per_block(b, carry):
            @pl.when(active(a, b))
            def _():
                total = dot3((ct[0], ct[1]), (sw[0, a, b], sw[1, a, b]))
                macc[b, 0] += total[:, :128]
                macc[b, 1] += total[:, 128:]

            return carry

        lax.fori_loop(0, 4, per_block, 0)

    def prepare(a, carry):
        def per_block(b, inner):
            @pl.when(active(a, b))
            def _():
                shift = 256 * (8 * a + r - 16 * b - c)
                block = jnp.where(row_iota + shift >= col_iota, adjoint_block(a, b), 0.0)
                sw[0, a, b], sw[1, a, b] = split(block)

            return inner

        lax.fori_loop(0, 4, per_block, 0)
        return carry

    for w in range(WAVES):
        pass_on(w)
        scattered(w)
        if w == WAVES - 1:
            column_send()
        gather_open(w)
    for w in range(WAVES):
        gather_first(w)
    column_open()
    load.wait()

    @pl.when(at_11)
    def _():
        rsend[...] = adjoint_block(0, 0)
        send(rsend, rblk.at[0], blk_sem.at[0], blk_sem.at[2], (0, 0))

    @pl.when(at_10)
    def _():
        rsend[...] = adjoint_block(0, 0)
        send(rsend, rblk.at[1], blk_sem.at[1], blk_sem.at[3], (0, 0))

    lax.fori_loop(0, 8, prepare, 0)
    for w in range(WAVES):
        gather_relay(w, 0)
        gather_relay(w, 1)
    column_relay()
    for w in range(WAVES):
        gather_relay(w, 2)
        gather_relay(w, 3)
    column_close()

    pair = lax.div(x, 2)
    for owner in (z, up(z), down(z)):
        mirrored(2 * owner + pair)
    for w in range(WAVES):
        gather_close(w)

    pivots = ((0, 0, 0), (1, 0, 1), (2, 1, 1))

    for slot, p, holder in pivots:

        @pl.when(r == holder)
        def _():
            src = crow.at[p, pl.ds(0, 2)]
            send(src, qbuf.at[slot], q_s.at[slot, 0], q_r.at[slot], (2 + holder, c))
            send(src, qbuf.at[slot], q_s.at[slot, 1], q_r.at[slot], (6 + holder, c))
            send(src, qbuf.at[slot], q_s.at[slot, 2], q_r.at[slot], (4 + holder, c))
            send(src, qbuf.at[slot], q_s.at[slot, 3], q_r.at[slot], mate)
            own = pltpu.make_async_copy(src, qbuf.at[slot], local_sem.at[1])
            own.start()
            own.wait()

    for step in range(4):
        mirrored(2 * step + 1 - pair)
    mirrored(2 * across_from(z) + pair)

    for b in range(4):
        post(
            macc.at[b, 1 - core], mate_in.at[b], mate_sem.at[0, b], mate_sem.at[1, b], mate
        )

    column_wait()

    def ready_columns(b, carry):
        for p in range(2):
            for half in range(2):
                high, low = split(ccol[b, half, p])
                rows, lanes = pl.ds(128 * half, 128), pl.ds(256 * p, 256)
                cc[0, b, rows, lanes] = high
                cc[1, b, rows, lanes] = low
        return carry

    lax.fori_loop(0, 4, ready_columns, 0)

    oacc[...] = jnp.zeros_like(oacc)

    def direct(a, carry):
        for p in range(2):

            @pl.when(c == p)
            def _():
                block = adjoint_block(a, 0)
                oacc[p, 2 * a] = -block[:128]
                oacc[p, 2 * a + 1] = -block[128:]

        def per_block(b, inner):
            @pl.when(active(a, b))
            def _():
                total = dot3((sw[0, a, b], sw[1, a, b]), (cc[0, b], cc[1, b]))
                for p in range(2):
                    for half in range(2):
                        oacc[p, 2 * a + half] += total[128 * half : 128 * half + 128, 256 * p : 256 * p + 256]

            return inner

        lax.fori_loop(0, 4, per_block, 0)
        return carry


    def ring_open(slot, held, pos, device, rows, opp, nbr, stage=None):
        def part(ref, half):
            return ref.at[pl.ds(rows * half, rows)]

        def go(src, dst, n, where):
            post(src, dst, ring.at[0, slot, n], ring.at[1, slot, n], device(where))

        if stage in (None, 0):
            far = held(across_from(pos))
            go(part(far, 0), opp.at[0], 0, down(pos))
            go(part(far, 1), opp.at[1], 1, up(pos))
        if stage in (None, 1):
            go(part(held(up(pos)), 0), part(nbr.at[1], 0), 3, up(pos))
        if stage in (None, 2):
            go(part(held(down(pos)), 1), part(nbr.at[0], 1), 2, down(pos))

    def ring_pass(slot, held, pos, device, rows, opp, nbr):
        def part(ref, half):
            return ref.at[pl.ds(rows * half, rows)]

        def go(src, dst, n, where):
            post(src, dst, ring.at[0, slot, n], ring.at[1, slot, n], device(where))

        arrived(opp.at[0], ring.at[1, slot, 0])
        mine = part(held(down(pos)), 0)
        mine[...] = mine[...] + opp[0]
        go(mine, part(nbr.at[0], 0), 4, down(pos))
        arrived(opp.at[1], ring.at[1, slot, 1])
        mine = part(held(up(pos)), 1)
        mine[...] = mine[...] + opp[1]
        go(mine, part(nbr.at[1], 1), 5, up(pos))

    def ring_close(slot, held, pos, device, rows, opp, nbr):
        def part(ref, half):
            return ref.at[pl.ds(rows * half, rows)]

        arrived(part(nbr.at[0], 1), ring.at[1, slot, 2])
        arrived(part(nbr.at[0], 0), ring.at[1, slot, 4])
        arrived(part(nbr.at[1], 0), ring.at[1, slot, 3])
        arrived(part(nbr.at[1], 1), ring.at[1, slot, 5])
        mine = held(pos)
        mine[...] = mine[...] + (nbr[0] + nbr[1])

    def first_ring(p, j):
        f, s = place[p]
        return (
            4 * p + j,
            lambda t: oacc.at[p, piece(p, j, t)],
            s,
            lambda t: member(p, f, t),
            64,
            opp1.at[p, j],
            nbr1.at[p, j],
        )

    def second_open(p):
        f, s = place[p]
        for n, hop in enumerate((across_from, up, down)):
            to = hop(f)
            post(
                oacc.at[p, piece(p, to, s)],
                near.at[p, n],
                ring2.at[0, p, n],
                ring2.at[1, p, n],
                member(p, to, s),
            )

    def second_close(p):
        for n in range(3):
            arrived(near.at[p, n], ring2.at[1, p, n])
        return oacc[p, c] + (near[p, 0] + (near[p, 1] + near[p, 2]))

    column_ring = (
        10,
        lambda t: macc.at[t, core],
        y,
        lambda t: (t * 2 + core, c),
        256,
        yopp,
        ynbr,
    )
    groups_of_rows = (across_from(z), up(z), down(z), z)
    for n, owner in enumerate(groups_of_rows):
        lax.fori_loop(2 * owner, 2 * owner + 2, direct, 0)
        ring_open(*first_ring(1, owner))
        if n < 3:
            for j in range(4):
                ring_open(*first_ring(0, j), stage=n)
    rings = [ring for n in range(4) for ring in (first_ring(0, n), first_ring(1, groups_of_rows[n]))]

    for b in range(4):
        arrived(mate_in.at[b], mate_sem.at[1, b])
    for b in range(4):
        mine = macc.at[b, core]
        mine[...] = mine[...] + mate_in[b]
    ring_open(*column_ring)

    for slot, p, holder in pivots:

        @pl.when(r != holder)
        def _():
            arrived(qbuf.at[slot], q_r.at[slot])

            @pl.when(core == holder)
            def _():
                send(qbuf.at[slot], qbuf.at[slot], q_s.at[slot, 3], q_r.at[slot], mate)

    def pivot(slot):
        return jnp.concatenate([qbuf[slot, 0], qbuf[slot, 1]], axis=0)

    def corners():
        return [qbuf[slot, h, :, 128 * h : 128 * h + 128] for slot in (0, 2) for h in range(2)]

    started = inverse_grow(inverse_open(corners()), corners(), (2, 4, 8))
    for n in range(4):
        qwork[n] = started[n]

    for spec in rings:
        ring_pass(*spec)
    ring_pass(*column_ring)

    grown = inverse_grow([qwork[n] for n in range(4)], corners(), (16, 32, 64))
    for n, slot in enumerate((0, 2)):
        first, second = grown[2 * n : 2 * n + 2]
        qinv[n, :128, :128] = first
        qinv[n, :128, 128:] = jnp.zeros_like(first)
        qinv[n, 128:, :128] = -exact(exact(second, qbuf[slot, 1, :, :128]), first)
        qinv[n, 128:, 128:] = second

    for spec in rings:
        ring_close(*spec)
    for p in range(2):
        second_open(p)
    ring_close(*column_ring)

    @pl.when(away)
    def _():
        send(macc.at[y, core], moved, moved_sem.at[0], moved_sem.at[1], target)

    @pl.when(jnp.logical_not(away))
    def _():
        moved[...] = macc[y, core]

    closed_0, closed_1 = second_close(0), second_close(1)

    @pl.when(from_away)
    def _():
        arrived(moved, moved_sem.at[1])

    keep = jnp.where(jnp.logical_and(c < 2, r < 2), 0.0, -1.0)
    extra = moved[...].T
    sums_1 = (closed_1 + extra[:, 256:]) * keep
    sums_0 = (closed_0 + extra[:, :256]) * keep
    parts_1, parts_0 = split(qinv[1]), split(qinv[0])
    solved_1 = times(sums_1, parts_1)
    apiece[1] = solved_1

    def pick(table, default):
        found = default
        for k, value in table.items():
            found = jnp.where(c == k, value, found)
        return found

    def hand_in(p):
        via = pick({k: v for k, (v, _) in relays[p].items()}, -1)
        slot = pick({k: n for k, (_, n) in relays[p].items()}, 0)

        @pl.when(via >= 0)
        def _():
            send(apiece.at[p], gstage.at[slot], ga_s.at[p], gst_r.at[slot], (r, via))

        @pl.when(jnp.logical_and(via < 0, c != p))
        def _():
            send(apiece.at[p], agath.at[c], ga_s.at[p], ga_r.at[c], (r, p))

    def hand_on():
        for p in range(2):
            for via, members in groups[p].items():

                @pl.when(c == via)
                def _():
                    for slot, k in enumerate(members):
                        arrived(gstage.at[slot], gst_r.at[slot])
                        send(gstage.at[slot], agath.at[k], gst_s.at[slot], ga_r.at[k], (r, p))

    hand_in(1)
    solved_0 = times(sums_0 - times(solved_1, pivot(1)), parts_0)
    apiece[0] = solved_0
    hand_in(0)

    sides_1, sides_0 = [tuple(v.T for v in split(m)) for m in (solved_1, solved_0)]
    right_1, right_0 = split(crow[1, c]), split(crow[0, c])
    for n, term in enumerate((dot3(sides_1, right_1), dot3(sides_1, right_0), dot3(sides_0, right_0))):
        for t in range(8):
            tpart[t, n] = term[32 * t : 32 * t + 32]
    for step in range(1, 8):
        to = lax.rem(r + step, 8)
        post(tpart.at[to], tin1.at[step], t1.at[0, step], t1.at[1, step], (to, c))
    result = tpart[r]
    for step in range(1, 8):
        arrived(tin1.at[step], t1.at[1, step])
        result = result + tin1[step]
    for t in range(4):
        tsum[t] = result[:, 8 * t : 8 * t + 8]
    for step in range(1, 4):
        to = lax.rem(x + step, 4)
        post(tsum.at[to], tin2.at[step], t2.at[0, step], t2.at[1, step], (r, 4 * z + to))
    result = tsum[x]
    for step in range(1, 4):
        arrived(tin2.at[step], t2.at[1, step])
        result = result + tin2[step]
    tslice[...] = result

    @pl.when(z != 0)
    def _():
        send(tslice, tin3.at[z], t3.at[0], t3.at[z], (r, x))

    @pl.when(z == 0)
    def _():
        total = result
        for n in range(1, 4):
            arrived(tin3.at[n], t3.at[n])
            total = total + tin3[n]
        tslice[...] = total

        @pl.when(jnp.logical_not(is_root))
        def _():
            send(tslice, tall.at[r, x], t3.at[0], troot.at[r, x], (0, 0))

    hand_on()

    def flat(parts):
        return jnp.concatenate(parts, axis=0)

    @pl.when(is_root)
    def _():
        tall[0, 0] = tslice[...]
        link = split(pivot(1))
        pivot_1, pivot_0 = turned(split(pivot(2))), turned(split(pivot(0)))
        ahead = split(times(link, parts_0))
        for t in range(8):
            for n in range(4):
                if t + n > 0:
                    arrived(tall.at[t, n], troot.at[t, n])
        arrived(rblk.at[0], blk_sem.at[2])
        arrived(rblk.at[1], blk_sem.at[3])

        def total(n):
            return flat([tall[t, m, n] for t in range(8) for m in range(4)])

        diag_1 = diag_step(pivot_1, parts_1, lower(rblk[0] - total(0)))
        rblk[0] = diag_1
        send(rblk.at[0], a01, blk_sem.at[6], blk_sem.at[5], (1, 1))
        rows_1 = times(rblk[1] - total(1), parts_0) - times(diag_1 + diag_1.T, ahead)
        rsend[...] = rows_1
        send(rsend, a01, blk_sem.at[4], blk_sem.at[5], (1, 0))
        sums = total(2) + times(turned(split(rows_1)), link)
        done[...] = diag_step(pivot_0, parts_0, lower(adjoint_block(0, 0) - sums))
        left(rsend, blk_sem.at[4])
        left(rblk.at[0], blk_sem.at[6])

    for p in range(2):

        @pl.when(c == p)
        def _():
            agath[p] = apiece[p]
            for k in range(16):
                if k != p:
                    arrived(agath.at[k], ga_r.at[k])

    @pl.when(jnp.logical_or(at_10, at_11))
    def _():
        arrived(a01, blk_sem.at[5])
        done[...] = a01[...]

    @pl.when(c < 2)
    def _():
        def write(k, carry):
            value = agath[k]
            for h in range(2):
                out[pl.ds(256 * k + h, 128, stride=2), :] = value[:, 128 * h : 128 * h + 128]
            return carry

        lax.fori_loop(0, 16, write, 0)

        @pl.when(jnp.logical_and(r < 2, jnp.logical_or(r == 1, c == 0)))
        def _():
            value = done[...]
            for h in range(2):
                out[pl.ds(h, 256, stride=2), :] = value[:, 128 * h : 128 * h + 128]

    @pl.when(c >= 2)
    def _():
        out[...] = jnp.zeros_like(out)

    for copy in pending:
        copy.wait_send()
    for p in range(2):

        @pl.when(c == p)
        def _():
            for k in orders[p]:
                for w in range(WAVES):
                    left(wave(panel.at[k], w), scat_s.at[k, w])

        @pl.when(c != p)
        def _():
            left(apiece.at[p], ga_s.at[p])

        for via, slot in relays[p].values():

            @pl.when(c == via)
            def _():
                for w in range(WAVES):
                    left(stage.at[slot, w], stage_s.at[slot, w])
                left(gstage.at[slot], gst_s.at[slot])

    @pl.when(from_away)
    def _():
        left(here, col_sem.at[0, 0])

    for slot, p, holder in pivots:

        @pl.when(core == holder)
        def _():
            left(qbuf.at[slot], q_s.at[slot, 3])

        @pl.when(r == holder)
        def _():
            for n in range(3):
                left(qbuf.at[slot], q_s.at[slot, n])

    @pl.when(at_11)
    def _():
        left(rsend, blk_sem.at[0])

    @pl.when(at_10)
    def _():
        left(rsend, blk_sem.at[1])

    @pl.when(away)
    def _():
        left(moved, moved_sem.at[0])

    @pl.when(jnp.logical_not(is_root))
    def _():
        left(tslice, t3.at[0])


def sweep(factor, adj):
    vmem = pltpu.VMEM
    dma = pltpu.SemaphoreType.DMA
    return pl.pallas_call(
        sweep_kernel,
        out_shape=jax.ShapeDtypeStruct((4096, 128), F32),
        in_specs=[pl.BlockSpec(memory_space=pl.ANY)] * 2,
        out_specs=pl.BlockSpec(memory_space=pltpu.VMEM),
        scratch_shapes=[
            vmem((16384, 128), F32),
            vmem((16, 128, 256), F32),
            vmem((2, 16, 128, 256), F32),
            vmem((4, 2, 2, 128, 256), F32),
            vmem((4, WAVES, 128 // WAVES, 256), F32),
            vmem((2, 512, 256), BF16),
            vmem((2, 8, 4, 256, 256), BF16),
            vmem((2, 4, 256, 512), BF16),
            vmem((2, 16, 128, 256), F32),
            vmem((4, 2, 512, 128), F32),
            vmem((4, 512, 128), F32),
            vmem((2, 256, 128), F32),
            vmem((2, 512, 128), F32),
            vmem((512, 128), F32),
            vmem((2, 4, 2, 64, 256), F32),
            vmem((2, 4, 2, 128, 256), F32),
            vmem((2, 3, 128, 256), F32),
            vmem((16, 128, 256), F32),
            vmem((4, 128, 256), F32),
            vmem((2, 128, 256), F32),
            vmem((3, 2, 128, 256), F32),
            vmem((2, 256, 256), F32),
            vmem((4, 128, 128), F32),
            vmem((8, 3, 32, 256), F32),
            vmem((8, 3, 32, 256), F32),
            vmem((4, 3, 8, 256), F32),
            vmem((4, 3, 8, 256), F32),
            vmem((3, 8, 256), F32),
            vmem((4, 3, 8, 256), F32),
            vmem((8, 4, 3, 8, 256), F32),
            vmem((2, 256, 256), F32),
            vmem((256, 256), F32),
            vmem((256, 256), F32),
            vmem((256, 256), F32),
            dma((10,)),
            dma((16, WAVES)),
            dma((2, WAVES)),
            dma((2, WAVES, 2, 4)),
            dma((2, WAVES, 2, 4, 4)),
            dma((4, WAVES)),
            dma((4, WAVES)),
            dma((2, 9)),
            dma((3, 4)),
            dma((3,)),
            dma((2, 11, 6)),
            dma((2, 2, 3)),
            dma((2, 4)),
            dma((2,)),
            dma((2,)),
            dma((16,)),
            dma((4,)),
            dma((4,)),
            dma((2, 8)),
            dma((2, 4)),
            dma((4,)),
            dma((8, 4)),
            dma((7,)),
        ],
        compiler_params=pltpu.CompilerParams(
            collective_id=0, has_side_effects=True, vmem_limit_bytes=60 * 2**20
        ),
        name="sweep",
    )(factor, adj)


def merge_kernel(adj, panel, out, held, solved, sem):
    r, c = lax.axis_index("row"), lax.axis_index("col")
    shape = (256, 8, 128)
    slot = lax.broadcasted_iota(jnp.int32, (1, 8, 128), 1)
    lane = lax.broadcasted_iota(jnp.int32, (1, 8, 128), 2)
    col = (16 * (slot // 2) + c) * 256 + lax.rem(slot, 2) * 128 + lane
    row = r * 256 + lax.broadcasted_iota(jnp.int32, shape, 0)

    def rows(ref, a):
        return ref.at[pl.ds(2048 * a, 2048)]

    def come(a):
        return pltpu.make_async_copy(rows(adj, a), held.at[a], sem.at[0, a])

    def go(a):
        return pltpu.make_async_copy(held.at[a], rows(out, a), sem.at[1, a])

    fetch = pltpu.make_async_copy(panel, solved, sem.at[2, 0])
    for a in range(8):
        come(a).start()

    @pl.when(c < 2)
    def _():
        fetch.start()
        fetch.wait()

    for a in range(8):
        come(a).wait()
        held[a] = jnp.where(row + 2048 * a >= col, held[a].reshape(shape), 0.0).reshape(2048, 128)

        @pl.when(c < 2)
        def _():
            for h in range(2):
                held[a, pl.ds(h, 256, stride=8), :] = solved[pl.ds(512 * a + h, 256, stride=2), :]

        go(a).start()
    for a in range(8):
        go(a).wait()


def merge(adj, panel):
    return pl.pallas_call(
        merge_kernel,
        out_shape=jax.ShapeDtypeStruct((16384, 128), F32),
        in_specs=[pl.BlockSpec(memory_space=pl.ANY)] * 2,
        out_specs=pl.BlockSpec(memory_space=pl.ANY),
        scratch_shapes=[
            pltpu.VMEM((8, 2048, 128), F32),
            pltpu.VMEM((4096, 128), F32),
            pltpu.SemaphoreType.DMA((3, 8)),
        ],
        compiler_params=pltpu.CompilerParams(vmem_limit_bytes=60 * 2**20),
        name="merge",
    )(adj, panel)


def shards(factor, adjoint):
    adj = adjoint.reshape(16384, 128)
    solved = sweep(factor.reshape(16384, 128), adj)
    return merge(adj, solved).reshape(adjoint.shape)


def solution(mesh):
    spec = P(None, "row", None, None, "col", None)
    return jax.shard_map(
        shards,
        mesh=mesh,
        in_specs=(spec, spec),
        out_specs=spec,
        check_vma=False,
    )
```

```python
import jax
import jax.numpy as jnp
from jax import lax
from jax.experimental import pallas as pl
from jax.experimental.pallas import tpu as pltpu
from jax.sharding import PartitionSpec as P

F32, BF16 = jnp.float32, jnp.bfloat16
MESH = pl.DeviceIdType.MESH
precise = lax.Precision.HIGHEST
WAVES = 1


def up(v):
    return lax.rem(v + 1, 4)


def down(v):
    return lax.rem(v + 3, 4)


def across_from(v):
    return lax.rem(v + 2, 4)


def split(value):
    high = value.astype(BF16)
    return high, (value - high.astype(F32)).astype(BF16)


def dot(left, right):
    return jnp.dot(left, right, preferred_element_type=F32)


def dot3(left, right):
    (left_high, left_low), (right_high, right_low) = left, right
    return dot(left_high, right_high) + (dot(left_high, right_low) + dot(left_low, right_high))


def exact(left, right):
    return jnp.dot(left, right, precision=precise, preferred_element_type=F32)


def iotas(shape):
    return (
        lax.broadcasted_iota(jnp.int32, shape, 0),
        lax.broadcasted_iota(jnp.int32, shape, 1),
    )


def lower(matrix):
    row, col = iotas(matrix.shape)
    return jnp.where(row >= col, matrix, 0.0)


def halve_diag(matrix):
    row, col = iotas(matrix.shape)
    return jnp.where(row > col, matrix, jnp.where(row == col, 0.5 * matrix, 0.0))


def inverse_open(blocks):
    row, col = iotas(blocks[0].shape)
    pair = jnp.logical_and(row // 2 == col // 2, row > col)
    found = []
    for q in blocks:
        diag = jnp.where(row == col, 1.0 / jnp.where(row == col, q, 1.0), 0.0)
        down_rows = jnp.sum(diag, axis=1, keepdims=True)
        down_cols = jnp.sum(diag, axis=0, keepdims=True)
        found.append(diag - jnp.where(pair, down_rows * q * down_cols, 0.0))
    return found


def inverse_grow(found, blocks, sizes):
    row, col = iotas(blocks[0].shape)
    for size in sizes:
        here = jnp.logical_and(row // (2 * size) == col // (2 * size), row // size > col // size)
        left = [exact(x, jnp.where(here, q, 0.0)) for x, q in zip(found, blocks)]
        found = [x - exact(y, x) for x, y in zip(found, left)]
    return found


def times(left, right):
    left_high, left_low = left if isinstance(left, tuple) else split(left)
    right_high, right_low = right if isinstance(right, tuple) else split(right)
    return dot(
        jnp.concatenate([left_low, left_high, left_high], axis=1),
        jnp.concatenate([right_high, right_low, right_high], axis=0),
    )


def turned(parts):
    return tuple(part.T for part in parts)


def diag_step(pivot, inverse, target):
    inner = halve_diag(times(pivot, target))
    return halve_diag(times(times(turned(inverse), inner), inverse))


def sweep_kernel(
    factor,
    adj,
    out,
    s_ref,
    panel,
    crow,
    ccol,
    stage,
    ct,
    sw,
    cc,
    oacc,
    macc,
    mate_in,
    yopp,
    ynbr,
    moved,
    opp1,
    nbr1,
    near,
    agath,
    gstage,
    apiece,
    qbuf,
    qinv,
    qwork,
    tpart,
    tin1,
    tsum,
    tin2,
    tslice,
    tin3,
    tall,
    rblk,
    rsend,
    done,
    a01,
    local_sem,
    scat_s,
    scat_r,
    ag1,
    ag2,
    stage_s,
    stage_r,
    col_sem,
    q_s,
    q_r,
    ring,
    ring2,
    mate_sem,
    moved_sem,
    ga_s,
    ga_r,
    gst_s,
    gst_r,
    t1,
    t2,
    t3,
    troot,
    blk_sem,
):
    r, c = lax.axis_index("row"), lax.axis_index("col")
    y, core = lax.div(r, 2), lax.rem(r, 2)
    z, x = lax.div(c, 4), lax.rem(c, 4)
    place = ((x, z), (z, x))
    home = lax.rem(c, 8)
    home_y, home_core = lax.div(home, 2), lax.rem(home, 2)
    group = lax.div(c, 8)
    mate = (y * 2 + 1 - core, c)
    target = (home, 4 * y + 2 * group + core)
    giver = (2 * z + lax.rem(x, 2), r + 8 * lax.div(x, 2))
    pending = []

    def piece(p, first, second):
        return second * 4 + first if p == 0 else first * 4 + second

    def member(p, first, second):
        return (r, piece(p, first, second))

    def send(src, dst, ss, rs, device):
        copy = pltpu.make_async_remote_copy(
            src_ref=src, dst_ref=dst, send_sem=ss, recv_sem=rs, device_id=device, device_id_type=MESH
        )
        copy.start()
        return copy

    def post(*args):
        pending.append(send(*args))

    def arrived(dst, rs):
        pltpu.make_async_remote_copy(
            src_ref=dst, dst_ref=dst, send_sem=rs, recv_sem=rs, device_id=mate, device_id_type=MESH
        ).wait_recv()

    def left(src, ss):
        pltpu.make_async_remote_copy(
            src_ref=src, dst_ref=src, send_sem=ss, recv_sem=ss, device_id=mate, device_id_type=MESH
        ).wait_send()

    holds_panel = c < 2

    def factor_part(n):
        part = pl.ds(4096 * n, 4096)
        return pltpu.make_async_copy(factor.at[part], s_ref.at[part], local_sem.at[2 + n])

    load = pltpu.make_async_copy(adj, s_ref, local_sem.at[0])

    @pl.when(holds_panel)
    def _():
        for n in range(4):
            factor_part(n).start()

    barrier = pltpu.get_barrier_semaphore()

    def greet(device):
        pl.semaphore_signal(barrier, inc=1, device_id=device, device_id_type=MESH)

    for step in range(1, 4):
        greet((r, 4 * z + lax.rem(x + step, 4)))
        greet((r, 4 * lax.rem(z + step, 4) + x))
    diagonal = ((4, 9), (12, 10), (12, 11), (5, 8), (13, 11), (13, 10))
    for one, other in diagonal:

        @pl.when(c == one)
        def _():
            greet((r, other))

        @pl.when(c == other)
        def _():
            greet((r, one))

    for step in range(1, 8):
        greet((lax.rem(r + step, 8), c))
    away = jnp.logical_or(target[0] != r, target[1] != c)
    from_away = jnp.logical_or(giver[0] != r, giver[1] != c)
    is_root = jnp.logical_and(r == 0, c == 0)
    owes_root = jnp.logical_and(r > 0, jnp.logical_and(c > 0, c < 4))
    at_11 = jnp.logical_and(r == 1, c == 1)
    at_10 = jnp.logical_and(r == 1, c == 0)

    @pl.when(from_away)
    def _():
        greet(giver)

    @pl.when(away)
    def _():
        greet(target)

    @pl.when(is_root)
    def _():
        for step in range(1, 8):
            for other in range(1, 4):
                greet((step, other))

    @pl.when(at_11)
    def _():
        greet((0, 0))

    @pl.when(holds_panel)
    def _():
        def take(k, carry):
            for h in range(2):
                panel[k, :, pl.ds(128 * h, 128)] = s_ref[pl.ds(k * 1024 + h, 128, stride=8), :]
            return carry

        for n in range(4):
            factor_part(n).wait()
            lax.fori_loop(4 * n, 4 * n + 4, take, 0)

    load.start()
    pl.semaphore_wait(
        barrier,
        13
        + sum(jnp.where(jnp.logical_or(c == one, c == other), 1, 0) for one, other in diagonal)
        + jnp.where(away, 1, 0)
        + jnp.where(from_away, 1, 0)
        + jnp.where(owes_root, 1, 0)
        + jnp.where(is_root, 1, 0),
    )

    orders = (
        (9, 10, 15, 8, 11, 7, 6, 14, 2, 5, 13, 3, 4, 12, 1),
        (8, 11, 14, 9, 10, 6, 7, 15, 3, 4, 12, 2, 5, 13, 0),
    )
    groups = (
        {4: (9, 8, 6, 5), 12: (10, 11, 14, 13), 3: (15, 7, 2)},
        {5: (8, 9, 7, 4), 13: (11, 10, 15, 12), 2: (14, 6, 3)},
    )
    relays = [
        {k: (via, slot) for via, members in g.items() for slot, k in enumerate(members)} for g in groups
    ]
    rows = 128 // WAVES

    def wave(ref, w):
        return ref.at[pl.ds(rows * w, rows)]

    for w in range(WAVES):
        for p in range(2):

            @pl.when(c == p)
            def _():
                for k in orders[p]:
                    src = wave(panel.at[k], w)
                    if k in relays[p]:
                        via, slot = relays[p][k]
                        send(src, stage.at[slot, w], scat_s.at[k, w], stage_r.at[slot, w], (r, via))
                    else:
                        send(src, wave(crow.at[p, k], w), scat_s.at[k, w], scat_r.at[p, w], (r, k))

    for p in range(2):

        @pl.when(c == p)
        def _():
            own = pltpu.make_async_copy(panel.at[p], crow.at[p, p], local_sem.at[1])
            own.start()
            own.wait()

    def pass_on(w):
        for p in range(2):
            for via, members in groups[p].items():

                @pl.when(c == via)
                def _():
                    for slot, k in enumerate(members):
                        held = stage.at[slot, w]
                        arrived(held, stage_r.at[slot, w])
                        send(held, wave(crow.at[p, k], w), stage_s.at[slot, w], scat_r.at[p, w], (r, k))

    def quarter(p, k, w, half):
        return crow.at[p, k, pl.ds(rows * w + rows // 2 * half, rows // 2)]

    def gather_second(p, w, q, first):
        f, s = place[p]
        held = wave(crow.at[p, piece(p, first, s)], w)
        post(held, held, ag2.at[0, w, p, q, 0], ag2.at[1, w, p, q, 0], member(p, f, up(s)))
        post(held, held, ag2.at[0, w, p, q, 1], ag2.at[1, w, p, q, 1], member(p, f, down(s)))

    def scattered(w):
        for p in range(2):

            @pl.when(c != p)
            def _():
                arrived(wave(crow.at[p, c], w), scat_r.at[p, w])

    def gather_open(w):
        for p in range(2):
            f, s = place[p]
            held = wave(crow.at[p, piece(p, f, s)], w)
            post(held, held, ag1.at[0, w, p, 0], ag1.at[1, w, p, 0], member(p, up(f), s))
            post(held, held, ag1.at[0, w, p, 1], ag1.at[1, w, p, 1], member(p, down(f), s))
            gather_second(p, w, 0, f)

    def gather_first(w):
        for p in range(2):
            f, s = place[p]
            k = piece(p, down(f), s)
            arrived(wave(crow.at[p, k], w), ag1.at[1, w, p, 0])
            part = quarter(p, k, w, 0)
            post(part, part, ag1.at[0, w, p, 2], ag1.at[1, w, p, 2], member(p, up(f), s))
            gather_second(p, w, 1, down(f))
            k = piece(p, up(f), s)
            arrived(wave(crow.at[p, k], w), ag1.at[1, w, p, 1])
            part = quarter(p, k, w, 1)
            post(part, part, ag1.at[0, w, p, 3], ag1.at[1, w, p, 3], member(p, down(f), s))
            gather_second(p, w, 2, up(f))
        for p in range(2):
            f, s = place[p]
            k = piece(p, across_from(f), s)
            arrived(quarter(p, k, w, 0), ag1.at[1, w, p, 2])
            arrived(quarter(p, k, w, 1), ag1.at[1, w, p, 3])
            gather_second(p, w, 3, across_from(f))

    def firsts(f):
        return f, down(f), up(f), across_from(f)

    def gather_relay(w, q):
        for p in range(2):
            f, s = place[p]
            first = firsts(f)[q]
            k = piece(p, first, down(s))
            arrived(wave(crow.at[p, k], w), ag2.at[1, w, p, q, 0])
            part = quarter(p, k, w, 0)
            post(part, part, ag2.at[0, w, p, q, 2], ag2.at[1, w, p, q, 2], member(p, f, up(s)))
            k = piece(p, first, up(s))
            arrived(wave(crow.at[p, k], w), ag2.at[1, w, p, q, 1])
            part = quarter(p, k, w, 1)
            post(part, part, ag2.at[0, w, p, q, 3], ag2.at[1, w, p, q, 3], member(p, f, down(s)))

    def gather_close(w):
        for q in range(4):
            for p in range(2):
                f, s = place[p]
                k = piece(p, firsts(f)[q], across_from(s))
                arrived(quarter(p, k, w, 0), ag2.at[1, w, p, q, 2])
                arrived(quarter(p, k, w, 1), ag2.at[1, w, p, q, 3])

    here = ccol.at[y, core]

    def to_mate(n, slot):
        post(slot, slot, col_sem.at[0, n], col_sem.at[1, n], mate)

    def column_send():
        own = crow.at[:, c]

        @pl.when(from_away)
        def _():
            send(own, ccol.at[z, lax.rem(x, 2)], col_sem.at[0, 0], col_sem.at[1, 0], giver)

        @pl.when(jnp.logical_not(from_away))
        def _():
            copy = pltpu.make_async_copy(own, here, local_sem.at[1])
            copy.start()
            copy.wait()

    def column_open():
        @pl.when(away)
        def _():
            arrived(here, col_sem.at[1, 0])

        post(here, here, col_sem.at[0, 1], col_sem.at[1, 1], (up(y) * 2 + core, c))
        post(here, here, col_sem.at[0, 2], col_sem.at[1, 2], (down(y) * 2 + core, c))
        to_mate(5, here)

    def column_relay():
        slot = ccol.at[down(y), core]
        arrived(slot, col_sem.at[1, 1])
        post(slot.at[0], slot.at[0], col_sem.at[0, 3], col_sem.at[1, 3], (up(y) * 2 + core, c))
        to_mate(6, slot)
        slot = ccol.at[up(y), core]
        arrived(slot, col_sem.at[1, 2])
        post(slot.at[1], slot.at[1], col_sem.at[0, 4], col_sem.at[1, 4], (down(y) * 2 + core, c))
        to_mate(7, slot)

    def column_close():
        slot = ccol.at[across_from(y), core]
        arrived(slot.at[0], col_sem.at[1, 3])
        arrived(slot.at[1], col_sem.at[1, 4])
        to_mate(8, slot)

    def column_wait():
        for n, t in ((5, y), (6, down(y)), (7, up(y)), (8, across_from(y))):
            arrived(ccol.at[t, 1 - core], col_sem.at[1, n])

    def adjoint_block(a, b):
        return jnp.concatenate(
            [s_ref[pl.ds(a * 2048 + 2 * b + h, 256, stride=8), :] for h in range(2)], axis=1
        )

    row_iota, col_iota = iotas((256, 256))

    def active(a, b):
        i, j = 8 * a + r, 16 * b + c
        return jnp.logical_and(j >= 2, j <= i)

    macc[...] = jnp.zeros_like(macc)

    def mirrored(a):
        for p in range(2):
            for half in range(2):
                high, low = split(crow[p, 2 * a + half])
                lanes = pl.ds(128 * half, 128)
                ct[0, pl.ds(256 * p, 256), lanes] = high.T
                ct[1, pl.ds(256 * p, 256), lanes] = low.T

        def per_block(b, carry):
            @pl.when(active(a, b))
            def _():
                total = dot3((ct[0], ct[1]), (sw[0, a, b], sw[1, a, b]))
                macc[b, 0] += total[:, :128]
                macc[b, 1] += total[:, 128:]

            return carry

        lax.fori_loop(0, 4, per_block, 0)

    def prepare(a, carry):
        def per_block(b, inner):
            @pl.when(active(a, b))
            def _():
                shift = 256 * (8 * a + r - 16 * b - c)
                block = jnp.where(row_iota + shift >= col_iota, adjoint_block(a, b), 0.0)
                sw[0, a, b], sw[1, a, b] = split(block)

            return inner

        lax.fori_loop(0, 4, per_block, 0)
        return carry

    for w in range(WAVES):
        pass_on(w)
        scattered(w)
        if w == WAVES - 1:
            column_send()
        gather_open(w)
    for w in range(WAVES):
        gather_first(w)
    column_open()
    load.wait()

    @pl.when(at_11)
    def _():
        rsend[...] = adjoint_block(0, 0)
        send(rsend, rblk.at[0], blk_sem.at[0], blk_sem.at[2], (0, 0))

    @pl.when(at_10)
    def _():
        rsend[...] = adjoint_block(0, 0)
        send(rsend, rblk.at[1], blk_sem.at[1], blk_sem.at[3], (0, 0))

    lax.fori_loop(0, 8, prepare, 0)
    for w in range(WAVES):
        gather_relay(w, 0)
        gather_relay(w, 1)
    column_relay()
    for w in range(WAVES):
        gather_relay(w, 2)
        gather_relay(w, 3)
    column_close()

    pair = lax.div(x, 2)
    for owner in (z, up(z), down(z)):
        mirrored(2 * owner + pair)
    for w in range(WAVES):
        gather_close(w)

    pivots = ((0, 0, 0), (1, 0, 1), (2, 1, 1))

    for slot, p, holder in pivots:

        @pl.when(r == holder)
        def _():
            src = crow.at[p, pl.ds(0, 2)]
            send(src, qbuf.at[slot], q_s.at[slot, 0], q_r.at[slot], (2 + holder, c))
            send(src, qbuf.at[slot], q_s.at[slot, 1], q_r.at[slot], (6 + holder, c))
            send(src, qbuf.at[slot], q_s.at[slot, 2], q_r.at[slot], (4 + holder, c))
            send(src, qbuf.at[slot], q_s.at[slot, 3], q_r.at[slot], mate)
            own = pltpu.make_async_copy(src, qbuf.at[slot], local_sem.at[1])
            own.start()
            own.wait()

    for step in range(4):
        mirrored(2 * step + 1 - pair)
    mirrored(2 * across_from(z) + pair)

    for b in range(4):
        post(
            macc.at[b, 1 - core], mate_in.at[b], mate_sem.at[0, b], mate_sem.at[1, b], mate
        )

    column_wait()

    def ready_columns(b, carry):
        for p in range(2):
            for half in range(2):
                high, low = split(ccol[b, half, p])
                rows, lanes = pl.ds(128 * half, 128), pl.ds(256 * p, 256)
                cc[0, b, rows, lanes] = high
                cc[1, b, rows, lanes] = low
        return carry

    lax.fori_loop(0, 4, ready_columns, 0)

    oacc[...] = jnp.zeros_like(oacc)

    def direct(a, carry):
        for p in range(2):

            @pl.when(c == p)
            def _():
                block = adjoint_block(a, 0)
                oacc[p, 2 * a] = -block[:128]
                oacc[p, 2 * a + 1] = -block[128:]

        def per_block(b, inner):
            @pl.when(active(a, b))
            def _():
                total = dot3((sw[0, a, b], sw[1, a, b]), (cc[0, b], cc[1, b]))
                for p in range(2):
                    for half in range(2):
                        oacc[p, 2 * a + half] += total[128 * half : 128 * half + 128, 256 * p : 256 * p + 256]

            return inner

        lax.fori_loop(0, 4, per_block, 0)
        return carry


    def ring_open(slot, held, pos, device, rows, opp, nbr, stage=None):
        def part(ref, half):
            return ref.at[pl.ds(rows * half, rows)]

        def go(src, dst, n, where):
            post(src, dst, ring.at[0, slot, n], ring.at[1, slot, n], device(where))

        if stage in (None, 0):
            far = held(across_from(pos))
            go(part(far, 0), opp.at[0], 0, down(pos))
            go(part(far, 1), opp.at[1], 1, up(pos))
        if stage in (None, 1):
            go(part(held(up(pos)), 0), part(nbr.at[1], 0), 3, up(pos))
        if stage in (None, 2):
            go(part(held(down(pos)), 1), part(nbr.at[0], 1), 2, down(pos))

    def ring_pass(slot, held, pos, device, rows, opp, nbr):
        def part(ref, half):
            return ref.at[pl.ds(rows * half, rows)]

        def go(src, dst, n, where):
            post(src, dst, ring.at[0, slot, n], ring.at[1, slot, n], device(where))

        arrived(opp.at[0], ring.at[1, slot, 0])
        mine = part(held(down(pos)), 0)
        mine[...] = mine[...] + opp[0]
        go(mine, part(nbr.at[0], 0), 4, down(pos))
        arrived(opp.at[1], ring.at[1, slot, 1])
        mine = part(held(up(pos)), 1)
        mine[...] = mine[...] + opp[1]
        go(mine, part(nbr.at[1], 1), 5, up(pos))

    def ring_close(slot, held, pos, device, rows, opp, nbr):
        def part(ref, half):
            return ref.at[pl.ds(rows * half, rows)]

        arrived(part(nbr.at[0], 1), ring.at[1, slot, 2])
        arrived(part(nbr.at[0], 0), ring.at[1, slot, 4])
        arrived(part(nbr.at[1], 0), ring.at[1, slot, 3])
        arrived(part(nbr.at[1], 1), ring.at[1, slot, 5])
        mine = held(pos)
        mine[...] = mine[...] + (nbr[0] + nbr[1])

    def first_ring(p, j):
        f, s = place[p]
        return (
            4 * p + j,
            lambda t: oacc.at[p, piece(p, j, t)],
            s,
            lambda t: member(p, f, t),
            64,
            opp1.at[p, j],
            nbr1.at[p, j],
        )

    def second_open(p):
        f, s = place[p]
        for n, hop in enumerate((across_from, up, down)):
            to = hop(f)
            post(
                oacc.at[p, piece(p, to, s)],
                near.at[p, n],
                ring2.at[0, p, n],
                ring2.at[1, p, n],
                member(p, to, s),
            )

    def second_close(p):
        for n in range(3):
            arrived(near.at[p, n], ring2.at[1, p, n])
        return oacc[p, c] + (near[p, 0] + (near[p, 1] + near[p, 2]))

    column_ring = (
        10,
        lambda t: macc.at[t, core],
        y,
        lambda t: (t * 2 + core, c),
        256,
        yopp,
        ynbr,
    )
    groups_of_rows = (across_from(z), up(z), down(z), z)
    for n, owner in enumerate(groups_of_rows):
        lax.fori_loop(2 * owner, 2 * owner + 2, direct, 0)
        ring_open(*first_ring(1, owner))
        if n < 3:
            for j in range(4):
                ring_open(*first_ring(0, j), stage=n)
    rings = [ring for n in range(4) for ring in (first_ring(0, n), first_ring(1, groups_of_rows[n]))]

    for b in range(4):
        arrived(mate_in.at[b], mate_sem.at[1, b])
    for b in range(4):
        mine = macc.at[b, core]
        mine[...] = mine[...] + mate_in[b]
    ring_open(*column_ring)

    for slot, p, holder in pivots:

        @pl.when(r != holder)
        def _():
            arrived(qbuf.at[slot], q_r.at[slot])

            @pl.when(core == holder)
            def _():
                send(qbuf.at[slot], qbuf.at[slot], q_s.at[slot, 3], q_r.at[slot], mate)

    def pivot(slot):
        return jnp.concatenate([qbuf[slot, 0], qbuf[slot, 1]], axis=0)

    def corners():
        return [qbuf[slot, h, :, 128 * h : 128 * h + 128] for slot in (0, 2) for h in range(2)]

    started = inverse_grow(inverse_open(corners()), corners(), (2, 4, 8))
    for n in range(4):
        qwork[n] = started[n]

    for spec in rings:
        ring_pass(*spec)
    ring_pass(*column_ring)

    grown = inverse_grow([qwork[n] for n in range(4)], corners(), (16, 32, 64))
    for n, slot in enumerate((0, 2)):
        first, second = grown[2 * n : 2 * n + 2]
        qinv[n, :128, :128] = first
        qinv[n, :128, 128:] = jnp.zeros_like(first)
        qinv[n, 128:, :128] = -exact(exact(second, qbuf[slot, 1, :, :128]), first)
        qinv[n, 128:, 128:] = second

    for spec in rings:
        ring_close(*spec)
    for p in range(2):
        second_open(p)
    ring_close(*column_ring)

    @pl.when(away)
    def _():
        send(macc.at[y, core], moved, moved_sem.at[0], moved_sem.at[1], target)

    @pl.when(jnp.logical_not(away))
    def _():
        moved[...] = macc[y, core]

    closed_0, closed_1 = second_close(0), second_close(1)

    @pl.when(from_away)
    def _():
        arrived(moved, moved_sem.at[1])

    keep = jnp.where(jnp.logical_and(c < 2, r < 2), 0.0, -1.0)
    extra = moved[...].T
    sums_1 = (closed_1 + extra[:, 256:]) * keep
    sums_0 = (closed_0 + extra[:, :256]) * keep
    parts_1, parts_0 = split(qinv[1]), split(qinv[0])
    solved_1 = times(sums_1, parts_1)
    apiece[1] = solved_1

    def pick(table, default):
        found = default
        for k, value in table.items():
            found = jnp.where(c == k, value, found)
        return found

    def hand_in(p):
        via = pick({k: v for k, (v, _) in relays[p].items()}, -1)
        slot = pick({k: n for k, (_, n) in relays[p].items()}, 0)

        @pl.when(via >= 0)
        def _():
            send(apiece.at[p], gstage.at[slot], ga_s.at[p], gst_r.at[slot], (r, via))

        @pl.when(jnp.logical_and(via < 0, c != p))
        def _():
            send(apiece.at[p], agath.at[c], ga_s.at[p], ga_r.at[c], (r, p))

    def hand_on(p):
        for via, members in groups[p].items():

            @pl.when(c == via)
            def _():
                for slot, k in enumerate(members):
                    arrived(gstage.at[slot], gst_r.at[slot])
                    send(gstage.at[slot], agath.at[k], gst_s.at[slot], ga_r.at[k], (r, p))

    hand_in(1)
    solved_0 = times(sums_0 - times(solved_1, pivot(1)), parts_0)
    apiece[0] = solved_0
    hand_in(0)

    sides_1, sides_0 = [tuple(v.T for v in split(m)) for m in (solved_1, solved_0)]
    right_1, right_0 = split(crow[1, c]), split(crow[0, c])
    for n, term in enumerate((dot3(sides_1, right_1), dot3(sides_1, right_0), dot3(sides_0, right_0))):
        for t in range(8):
            tpart[t, n] = term[32 * t : 32 * t + 32]
    for step in range(1, 8):
        to = lax.rem(r + step, 8)
        post(tpart.at[to], tin1.at[step], t1.at[0, step], t1.at[1, step], (to, c))
    hand_on(1)
    result = tpart[r]
    for step in range(1, 8):
        arrived(tin1.at[step], t1.at[1, step])
        result = result + tin1[step]
    for t in range(4):
        tsum[t] = result[:, 8 * t : 8 * t + 8]
    for step in range(1, 4):
        to = lax.rem(x + step, 4)
        post(tsum.at[to], tin2.at[step], t2.at[0, step], t2.at[1, step], (r, 4 * z + to))
    result = tsum[x]
    for step in range(1, 4):
        arrived(tin2.at[step], t2.at[1, step])
        result = result + tin2[step]
    tslice[...] = result

    @pl.when(z != 0)
    def _():
        send(tslice, tin3.at[z], t3.at[0], t3.at[z], (r, x))

    @pl.when(z == 0)
    def _():
        total = result
        for n in range(1, 4):
            arrived(tin3.at[n], t3.at[n])
            total = total + tin3[n]
        tslice[...] = total

        @pl.when(jnp.logical_not(is_root))
        def _():
            send(tslice, tall.at[r, x], t3.at[0], troot.at[r, x], (0, 0))

    hand_on(0)

    def flat(parts):
        return jnp.concatenate(parts, axis=0)

    @pl.when(is_root)
    def _():
        tall[0, 0] = tslice[...]
        link = split(pivot(1))
        pivot_1, pivot_0 = turned(split(pivot(2))), turned(split(pivot(0)))
        ahead = turned(split(times(link, parts_0)))
        for t in range(8):
            for n in range(4):
                if t + n > 0:
                    arrived(tall.at[t, n], troot.at[t, n])
        arrived(rblk.at[0], blk_sem.at[2])
        arrived(rblk.at[1], blk_sem.at[3])

        def total(n):
            return flat([tall[t, m, n] for t in range(8) for m in range(4)])

        diag_1 = diag_step(pivot_1, parts_1, lower(rblk[0] - total(0)))
        rblk[0] = diag_1
        send(rblk.at[0], a01, blk_sem.at[6], blk_sem.at[5], (1, 1))
        known = times(rblk[1] - total(1), parts_0)
        rest = lower(adjoint_block(0, 0) - total(2) - times(turned(split(known)), link))
        linked = split(times(diag_1 + diag_1.T, link))
        rsend[...] = known - times(linked, parts_0)
        send(rsend, a01, blk_sem.at[4], blk_sem.at[5], (1, 0))
        done[...] = diag_step(pivot_0, parts_0, rest + lower(times(ahead, linked)))
        left(rsend, blk_sem.at[4])
        left(rblk.at[0], blk_sem.at[6])

    for p in range(2):

        @pl.when(c == p)
        def _():
            agath[p] = apiece[p]
            for k in range(16):
                if k != p:
                    arrived(agath.at[k], ga_r.at[k])

    @pl.when(jnp.logical_or(at_10, at_11))
    def _():
        arrived(a01, blk_sem.at[5])
        done[...] = a01[...]

    @pl.when(c < 2)
    def _():
        def write(k, carry):
            value = agath[k]
            for h in range(2):
                out[pl.ds(256 * k + h, 128, stride=2), :] = value[:, 128 * h : 128 * h + 128]
            return carry

        lax.fori_loop(0, 16, write, 0)

        @pl.when(jnp.logical_and(r < 2, jnp.logical_or(r == 1, c == 0)))
        def _():
            value = done[...]
            for h in range(2):
                out[pl.ds(h, 256, stride=2), :] = value[:, 128 * h : 128 * h + 128]

    @pl.when(c >= 2)
    def _():
        out[...] = jnp.zeros_like(out)

    for copy in pending:
        copy.wait_send()
    for p in range(2):

        @pl.when(c == p)
        def _():
            for k in orders[p]:
                for w in range(WAVES):
                    left(wave(panel.at[k], w), scat_s.at[k, w])

        @pl.when(c != p)
        def _():
            left(apiece.at[p], ga_s.at[p])

        for via, slot in relays[p].values():

            @pl.when(c == via)
            def _():
                for w in range(WAVES):
                    left(stage.at[slot, w], stage_s.at[slot, w])
                left(gstage.at[slot], gst_s.at[slot])

    @pl.when(from_away)
    def _():
        left(here, col_sem.at[0, 0])

    for slot, p, holder in pivots:

        @pl.when(core == holder)
        def _():
            left(qbuf.at[slot], q_s.at[slot, 3])

        @pl.when(r == holder)
        def _():
            for n in range(3):
                left(qbuf.at[slot], q_s.at[slot, n])

    @pl.when(at_11)
    def _():
        left(rsend, blk_sem.at[0])

    @pl.when(at_10)
    def _():
        left(rsend, blk_sem.at[1])

    @pl.when(away)
    def _():
        left(moved, moved_sem.at[0])

    @pl.when(jnp.logical_not(is_root))
    def _():
        left(tslice, t3.at[0])


def sweep(factor, adj):
    vmem = pltpu.VMEM
    dma = pltpu.SemaphoreType.DMA
    return pl.pallas_call(
        sweep_kernel,
        out_shape=jax.ShapeDtypeStruct((4096, 128), F32),
        in_specs=[pl.BlockSpec(memory_space=pl.ANY)] * 2,
        out_specs=pl.BlockSpec(memory_space=pltpu.VMEM),
        scratch_shapes=[
            vmem((16384, 128), F32),
            vmem((16, 128, 256), F32),
            vmem((2, 16, 128, 256), F32),
            vmem((4, 2, 2, 128, 256), F32),
            vmem((4, WAVES, 128 // WAVES, 256), F32),
            vmem((2, 512, 256), BF16),
            vmem((2, 8, 4, 256, 256), BF16),
            vmem((2, 4, 256, 512), BF16),
            vmem((2, 16, 128, 256), F32),
            vmem((4, 2, 512, 128), F32),
            vmem((4, 512, 128), F32),
            vmem((2, 256, 128), F32),
            vmem((2, 512, 128), F32),
            vmem((512, 128), F32),
            vmem((2, 4, 2, 64, 256), F32),
            vmem((2, 4, 2, 128, 256), F32),
            vmem((2, 3, 128, 256), F32),
            vmem((16, 128, 256), F32),
            vmem((4, 128, 256), F32),
            vmem((2, 128, 256), F32),
            vmem((3, 2, 128, 256), F32),
            vmem((2, 256, 256), F32),
            vmem((4, 128, 128), F32),
            vmem((8, 3, 32, 256), F32),
            vmem((8, 3, 32, 256), F32),
            vmem((4, 3, 8, 256), F32),
            vmem((4, 3, 8, 256), F32),
            vmem((3, 8, 256), F32),
            vmem((4, 3, 8, 256), F32),
            vmem((8, 4, 3, 8, 256), F32),
            vmem((2, 256, 256), F32),
            vmem((256, 256), F32),
            vmem((256, 256), F32),
            vmem((256, 256), F32),
            dma((10,)),
            dma((16, WAVES)),
            dma((2, WAVES)),
            dma((2, WAVES, 2, 4)),
            dma((2, WAVES, 2, 4, 4)),
            dma((4, WAVES)),
            dma((4, WAVES)),
            dma((2, 9)),
            dma((3, 4)),
            dma((3,)),
            dma((2, 11, 6)),
            dma((2, 2, 3)),
            dma((2, 4)),
            dma((2,)),
            dma((2,)),
            dma((16,)),
            dma((4,)),
            dma((4,)),
            dma((2, 8)),
            dma((2, 4)),
            dma((4,)),
            dma((8, 4)),
            dma((7,)),
        ],
        compiler_params=pltpu.CompilerParams(
            collective_id=0, has_side_effects=True, vmem_limit_bytes=60 * 2**20
        ),
        name="sweep",
    )(factor, adj)


def merge_kernel(adj, panel, out, held, solved, sem):
    r, c = lax.axis_index("row"), lax.axis_index("col")
    shape = (256, 8, 128)
    slot = lax.broadcasted_iota(jnp.int32, (1, 8, 128), 1)
    lane = lax.broadcasted_iota(jnp.int32, (1, 8, 128), 2)
    col = (16 * (slot // 2) + c) * 256 + lax.rem(slot, 2) * 128 + lane
    row = r * 256 + lax.broadcasted_iota(jnp.int32, shape, 0)

    def rows(ref, a):
        return ref.at[pl.ds(2048 * a, 2048)]

    def come(a):
        return pltpu.make_async_copy(rows(adj, a), held.at[a], sem.at[0, a])

    def go(a):
        return pltpu.make_async_copy(held.at[a], rows(out, a), sem.at[1, a])

    fetch = pltpu.make_async_copy(panel, solved, sem.at[2, 0])
    for a in range(8):
        come(a).start()

    @pl.when(c < 2)
    def _():
        fetch.start()
        fetch.wait()

    for a in range(8):
        come(a).wait()
        held[a] = jnp.where(row + 2048 * a >= col, held[a].reshape(shape), 0.0).reshape(2048, 128)

        @pl.when(c < 2)
        def _():
            for h in range(2):
                held[a, pl.ds(h, 256, stride=8), :] = solved[pl.ds(512 * a + h, 256, stride=2), :]

        go(a).start()
    for a in range(8):
        go(a).wait()


def merge(adj, panel):
    return pl.pallas_call(
        merge_kernel,
        out_shape=jax.ShapeDtypeStruct((16384, 128), F32),
        in_specs=[pl.BlockSpec(memory_space=pl.ANY)] * 2,
        out_specs=pl.BlockSpec(memory_space=pl.ANY),
        scratch_shapes=[
            pltpu.VMEM((8, 2048, 128), F32),
            pltpu.VMEM((4096, 128), F32),
            pltpu.SemaphoreType.DMA((3, 8)),
        ],
        compiler_params=pltpu.CompilerParams(vmem_limit_bytes=60 * 2**20),
        name="merge",
    )(adj, panel)


def shards(factor, adjoint):
    adj = adjoint.reshape(16384, 128)
    solved = sweep(factor.reshape(16384, 128), adj)
    return merge(adj, solved).reshape(adjoint.shape)


def solution(mesh):
    spec = P(None, "row", None, None, "col", None)
    return jax.shard_map(
        shards,
        mesh=mesh,
        in_specs=(spec, spec),
        out_specs=spec,
        check_vma=False,
    )
```
